1024 devices in a mesh: gx: 64 (over y, x, core), gy: 16 (over z).
Axes of the slice: x: 4, y: 8, z: 16, core: 2. Of those that a mesh axis runs over, the one named last changes fastest.
Arguments:
- density: int32 [256, 128, 512], P('gx', 'gy'), may hold values from 0 to 255
- fixed: int32 [256, 128, 512], P('gx', 'gy'), may hold values from 0 to 1
- loaded: int32 [256, 128, 512], P('gx', 'gy'), may hold values 0 or 1
- load: float32 [3, 256, 128, 512], P(None, 'gx', 'gy'), may hold values from -6 to 6
Outputs:
- correction: float32 [3, 256, 128, 512], P(None, 'gx', 'gy')
The draws below stay inside these ranges and needn't reach their ends.
All inputs are finite; a program needn't handle non-finite values. No bound on the sum of `loaded` on one device may be relied on, other than what follows from the above.
Results may differ from the reference program's by a relative error of at most 0.0001.
Values sent between devices are 32-bit elements; how exact they have to be, the bound alone decides.
No kernel may reach another device: no remote copies, remote signals or barrier semaphores. Data moves between devices by JAX's collectives and lax.ppermute only.
A program may use at most 64 MiB of HBM per device.

```python
import jax
import jax.numpy as jnp
from jax import lax

NZ = 512
SWEEPS = 4
NX = 256
NY = 128


def draw_fixed(key, part):
    key = jax.random.fold_in(key, 11)
    subkeys = jax.random.split(key, 8)
    shape = (NX, NY, NZ)
    first_index = lax.broadcasted_iota(jnp.int32, shape, 0)
    second_index = lax.broadcasted_iota(jnp.int32, shape, 1)
    third_index = lax.broadcasted_iota(jnp.int32, shape, 2)
    scatter = jax.random.randint(subkeys[0], shape, 0, 32) == 0
    clamped = jnp.logical_or(scatter, first_index == 0)
    wide_x = max(4, NX // 16 * 4)
    wide_y = max(4, NY // 16 * 4)
    wide_z = max(4, NZ // 8 * 4)
    for box_number in range(6):
        box_keys = jax.random.split(subkeys[box_number + 1], 6)
        if box_number % 2 == 0:
            start_x = jax.random.randint(box_keys[0], (), 0, (NX - wide_x) // 4 + 1) * 4
            start_y = jax.random.randint(box_keys[1], (), 0, (NY - wide_y) // 4 + 1) * 4
            start_z = jax.random.randint(box_keys[2], (), 0, (NZ - wide_z) // 4 + 1) * 4
            span_x = wide_x
            span_y = wide_y
            span_z = wide_z
        else:
            start_x = jax.random.randint(box_keys[0], (), 0, NX - wide_x + 1)
            start_y = jax.random.randint(box_keys[1], (), 0, NY - wide_y + 1)
            start_z = jax.random.randint(box_keys[2], (), 0, NZ - wide_z + 1)
            span_x = jax.random.randint(box_keys[3], (), wide_x // 2, wide_x + 1)
            span_y = jax.random.randint(box_keys[4], (), wide_y // 2, wide_y + 1)
            span_z = jax.random.randint(box_keys[5], (), wide_z // 2, wide_z + 1)
        inside = (first_index >= start_x) & (first_index < start_x + span_x)
        inside = inside & (second_index >= start_y) & (second_index < start_y + span_y)
        inside = inside & (third_index >= start_z) & (third_index < start_z + span_z)
        clamped = jnp.logical_or(clamped, inside)
    return clamped.astype(jnp.int32)


def touch_ends(values, rng, least, largest):
    longest = values.shape.index(max(values.shape))
    spots = []
    for shift in (0, 1):
        where = [jax.random.randint(jax.random.fold_in(rng, axis), (), 0, length) for axis, length in enumerate(values.shape)]
        where[longest] = (where[longest] + shift) % values.shape[longest]
        spots.append(tuple(where))
    return values.at[spots[0]].set(least).at[spots[1]].set(largest)


def block_levels(own_key, shape, cuts, smallest, top_value):
    def one(position, shards_of):
        heights = jax.random.uniform(jax.random.fold_in(jax.random.fold_in(own_key, 6), position), (shards_of,), jnp.float32, smallest / len(cuts), top_value / len(cuts))
        return jnp.repeat(jnp.exp(heights), shape[position] // shards_of).reshape((-1,) + (1,) * (len(shape) - position - 1))

    loudness = one(*cuts[0])
    for cut in cuts[1:]:
        loudness = loudness * one(*cut)
    return loudness


def scatter_about(key, extent, scale, reach, cuts=(), dtype=jnp.bfloat16):
    array = jax.random.normal(key, extent, jnp.float32) * scale
    if len(cuts) > 0:
        array = block_levels(key, extent, cuts, -0.22, 0.18) * array
    return jnp.clip(array, min=-reach, max=reach).astype(dtype)


def setup_inputs(seed: int = 0) -> dict:
    streams_of = jax.random.split(jax.random.key(seed), 5)
    return {
        "density": touch_ends(jax.random.randint(streams_of[0], (NX, NY, NZ), 0, 256), jax.random.fold_in(streams_of[0], 1), 0, 255).astype(jnp.int32),
        "fixed": draw_fixed(jax.random.fold_in(streams_of[4], 71), 0),
        "loaded": touch_ends((jax.random.randint(streams_of[2], (NX, NY, NZ), 0, 2) < 1).astype(jnp.int32), jax.random.fold_in(streams_of[2], 1), 0, 1),
        "load": scatter_about(streams_of[3], (3, NX, NY, NZ), 1.0, 6.0, ((1, 64), (2, 16)), jnp.float32),
    }


COUPLING = 0.25
DAMPING = 0.8


def neighbour_offsets():
    result = []
    for shift_x in (-1, 0, 1):
        for shift_y in (-1, 0, 1):
            for shift_z in (-1, 0, 1):
                if (shift_x, shift_y, shift_z) != (0, 0, 0):
                    result.append((shift_x, shift_y, shift_z))
    return result


def stencil(padded, scale):
    a = padded.shape[1] - 2
    b = padded.shape[2] - 2
    c = padded.shape[3] - 2
    centre = padded[:, 1:a + 1, 1:b + 1, 1:c + 1]
    stiff = centre[3]
    parts = [0.1 * stiff * centre[first] for first in range(3)]
    for offset in neighbour_offsets():
        count = sum(1 for value in offset if value != 0)
        weight = 0.5 ** (count - 1)
        near = padded[:, 1 + offset[0]:1 + offset[0] + a, 1 + offset[1]:1 + offset[1] + b, 1 + offset[2]:1 + offset[2] + c]
        couple = weight * 0.5 * (stiff + near[3])
        for first in range(3):
            term = centre[first] - near[first]
            for second in range(3):
                if second != first and offset[first] * offset[second] != 0:
                    term = term - COUPLING * offset[first] * offset[second] * near[second]
            parts[first] = parts[first] + couple * term
    return scale * jnp.stack(parts)


def block_sum(field):
    k, a, b, c = field.shape
    return field.reshape(k, a // 2, 2, b // 2, 2, c // 2, 2).sum(axis=(2, 4, 6))


def block_max(field):
    k, a, b, c = field.shape
    return field.reshape(k, a // 2, 2, b // 2, 2, c // 2, 2).max(axis=(2, 4, 6))


def prolong(field):
    return jnp.repeat(jnp.repeat(jnp.repeat(field, 2, axis=1), 2, axis=2), 2, axis=3)


def pad_zero(stacked):
    return jnp.pad(stacked, ((0, 0), (1, 1), (1, 1), (1, 1)))


def first_step(force, stiff, free, scale):
    return free * DAMPING * force / (scale * (7.1 * stiff + 7.5))


def smooth(update, force, stiff, free, scale):
    image = stencil(pad_zero(jnp.concatenate([update, stiff])), scale)
    return update + free * DAMPING * (force - image) / (scale * (7.1 * stiff + 7.5))


def residual_of(update, force, stiff, free, scale):
    image = stencil(pad_zero(jnp.concatenate([update, stiff])), scale)
    return free * (force - image)


def reference(density, fixed, loaded, load):
    level = (density.astype(jnp.float32) + 1.0) / 256.0
    stiff_fine = (0.05 + level * level * level)[None]
    free_fine = (1 - fixed).astype(jnp.float32)[None]
    force_fine = free_fine * loaded.astype(jnp.float32)[None] * load
    stiff_mid = block_sum(stiff_fine) / 8.0
    free_mid = block_max(free_fine)
    stiff_low = block_sum(stiff_mid) / 8.0
    free_low = block_max(free_mid)
    fine_update = first_step(force_fine, stiff_fine, free_fine, 1.0)
    force_mid = block_sum(residual_of(fine_update, force_fine, stiff_fine, free_fine, 1.0))
    mid_update = first_step(force_mid, stiff_mid, free_mid, 2.0)
    force_low = block_sum(residual_of(mid_update, force_mid, stiff_mid, free_mid, 2.0))
    low_update = first_step(force_low, stiff_low, free_low, 4.0)
    for sweep in range(SWEEPS - 1):
        low_update = smooth(low_update, force_low, stiff_low, free_low, 4.0)
    mid_update = mid_update + free_mid * prolong(low_update)
    mid_update = smooth(mid_update, force_mid, stiff_mid, free_mid, 2.0)
    fine_update = fine_update + free_fine * prolong(mid_update)
    return smooth(fine_update, force_fine, stiff_fine, free_fine, 1.0)
```

```python
import jax
import jax.numpy as jnp
from jax import lax
from jax.experimental import pallas as pl
from jax.experimental.pallas import tpu as pltpu
from jax.sharding import PartitionSpec as P

F32 = jnp.float32
VMEM = pl.BlockSpec(memory_space=pltpu.VMEM)
PARAMS = pltpu.CompilerParams(vmem_limit_bytes=48 * 1024 * 1024)


def iota(shape, dim):
    return lax.broadcasted_iota(jnp.int32, shape, dim)


def exact_dot(a, b):
    return jnp.dot(a, b, precision=lax.Precision.HIGHEST, preferred_element_type=F32)


def pool_matrix(n):
    shape = (n, n // 2)
    return (iota(shape, 0) // 2 == iota(shape, 1)).astype(F32)


def spread_matrix(n):
    shape = (n, 2 * n)
    return (iota(shape, 0) == iota(shape, 1) // 2).astype(F32)


def z_parts(tiles):
    t, d = [], []
    for a in tiles:
        n = a.shape[1]
        lane = iota(a.shape, 1)
        after = jnp.where(lane == n - 1, 0.0, pltpu.roll(a, n - 1, 1))
        before = jnp.where(lane == 0, 0.0, pltpu.roll(a, 1, 1))
        t.append((after + before) + 2.0 * a)
        d.append(after - before)
    return tuple(t), tuple(d)


def y_pair(tiles):
    a = tiles[0]
    n = a.shape[0]
    if len(tiles) == 1:
        return pltpu.roll(a, n - 1, 0), pltpu.roll(a, 1, 0)
    row = iota(a.shape, 0)
    after = pltpu.roll(jnp.where(row == 0, tiles[1], a), n - 1, 0)
    before = pltpu.roll(jnp.where(row == n - 1, tiles[1], a), 1, 0)
    return after, before


def y_t(tiles):
    after, before = y_pair(tiles)
    return (after + before) + 2.0 * tiles[0]


def y_d(tiles):
    after, before = y_pair(tiles)
    return after - before


def y_both(tiles):
    after, before = y_pair(tiles)
    return (after + before) + 2.0 * tiles[0], after - before


def plane_terms(v):
    (tx, dx), (ty, dy), (tz, dz) = [z_parts(c) for c in v]
    xt, xd = y_both(tx)
    xc = y_t(dx)
    yt, yd = y_both(ty)
    yc = y_d(dy)
    zt = y_t(tz)
    zb, zc = y_both(dz)
    return (
        (xt, yt + 0.25 * zc, zt + 0.25 * yc),
        (0.25 * (yd + zb), 0.25 * xd, 0.25 * xc),
    )


def scalar_terms(s):
    t, _ = z_parts(s)
    return y_t(t)


def times(a, b):
    return tuple(p * q for p, q in zip(a, b))


def stiff_sums(s, planes):
    terms = {p: scalar_terms(s[p]) for p in range(planes[0] - 1, planes[-1] + 2)}
    return {p: 2.0 * terms[p] + (terms[p + 1] + terms[p - 1]) for p in planes}


def stencil(v, s, sums, planes):
    own, scaled = {}, {}
    result = {}
    for p in range(planes[0] - 1, planes[-1] + 2):
        for store, field in ((own, v[p]), (scaled, [times(c, s[p]) for c in v[p]])):
            even, odd = plane_terms(field)
            store[p] = (
                [2.0 * e for e in even],
                [e + o for e, o in zip(even, odd)],
                [e - o for e, o in zip(even, odd)],
            )
        q = p - 1
        if q in planes:
            here = []
            for c in range(3):
                plain = own[q][0][c] + (own[q + 1][1][c] + own[q - 1][2][c])
                heavy = scaled[q][0][c] + (scaled[q + 1][1][c] + scaled[q - 1][2][c])
                u, k = v[q][c][0], s[q][0]
                here.append(8.1 * (k * u) + 0.125 * (u * sums[q] - (k * plain + heavy)))
            result[q] = here
    return result


def gain(stiff, free):
    return free * 0.8 / (7.1 * stiff + 7.5)


def prepare_kernel(density, fixed, loaded, load, fine, low_side, high_side):
    for p in range(4):
        level = (density[p].astype(F32) + 1.0) * (1.0 / 256.0)
        stiff = 0.05 + level * level * level
        free = (1 - fixed[p]).astype(F32)
        factor = gain(stiff, free) * loaded[p].astype(F32)
        values = [factor * load[c, p] for c in range(3)] + [stiff, free]
        for f in range(5):
            fine[f, p] = values[f]
            if p == 0:
                low_side[f] = values[f]
            if p == 3:
                high_side[f] = values[f]


def fine_tiles(fine, before, after, row_before, row_after):
    row = iota((8, fine.shape[3]), 0)
    result = []
    for p in range(6):
        here = []
        for f in range(5):
            main = before[f] if p == 0 else after[f] if p == 5 else fine[f, p - 1]
            rim = jnp.where(
                row == 0, row_after[f, pl.ds(p, 1), :], row_before[f, pl.ds(p, 1), :]
            )
            here.append((main, rim))
        result.append(here)
    return result


def fine_residual_kernel(fine, before, after, row_before, row_after, mid):
    tiles = fine_tiles(fine, before, after, row_before, row_after)
    v = [t[:3] for t in tiles]
    s = [t[3] for t in tiles]
    planes = range(1, 5)
    image = stencil(v, s, stiff_sums(s, planes), planes)
    rows = [[], [], [], [], []]
    for p in planes:
        stiff, free = s[p][0], tiles[p][4][0]
        back = 1.25 * (7.1 * stiff + 7.5)
        for c in range(3):
            rows[c].append(free * (back * v[p][c][0] - image[p][c]))
        rows[3].append(stiff)
        rows[4].append(free)
    pairs = []
    for f in range(5):
        pairs += [rows[f][0] + rows[f][1], rows[f][2] + rows[f][3]]
    wide = jnp.concatenate(pairs, axis=0)
    short = exact_dot(wide, pool_matrix(wide.shape[1]))
    shape = (40, 80)
    left = (iota(shape, 0) == iota(shape, 1) // 2).astype(F32)
    sums = exact_dot(left, short)
    mid[0:24] = sums[0:24]
    mid[24:32] = sums[24:32] * 0.125
    mid[32:40] = (sums[32:40] > 0.5).astype(F32)


def mid_fields(mid):
    v, s, free, gains = [], [], [], []
    for p in range(6):
        stiff, open_ = mid[3, p], mid[4, p]
        g = gain(stiff, open_)
        v.append([(0.5 * g * mid[c, p],) for c in range(3)])
        s.append((stiff,))
        free.append(open_)
        gains.append(g)
    return v, s, free, gains


def mid_residual_kernel(mid, low):
    v, s, free, _ = mid_fields(mid)
    planes = range(2, 4)
    image = stencil(v, s, stiff_sums(s, planes), planes)
    pairs = []
    for c in range(3):
        pairs.append(
            sum(free[p] * (mid[c, p] - 2.0 * image[p][c]) for p in planes)
        )
    pairs.append(s[2][0] + s[3][0])
    pairs.append(free[2] + free[3])
    wide = jnp.concatenate(pairs, axis=0)
    short = exact_dot(wide, pool_matrix(wide.shape[1]))
    shape = (10, 40)
    out, source = iota(shape, 0), iota(shape, 1)
    left = (source // 8 == out // 2) & (source % 8 // 2 == 1 + out % 2)
    sums = exact_dot(left.astype(F32), short)
    low[0:6] = sums[0:6]
    low[6:8] = sums[6:8] * 0.125
    low[8:10] = (sums[8:10] > 0.5).astype(F32)


def finish_kernel(low, mid, fine, before, after, row_before, row_after, out):
    s = [(low[3, p],) for p in range(9)]
    gains = [gain(low[3, p], low[4, p]) for p in range(9)]
    first = [[0.25 * gains[p] * low[c, p] for c in range(3)] for p in range(9)]
    v = {p: [(c,) for c in first[p]] for p in range(9)}
    sums = stiff_sums(s, range(1, 8))
    for reach in (1, 2, 3):
        planes = range(reach, 9 - reach)
        image = stencil(v, s, sums, planes)
        v = {
            p: [
                (v[p][c][0] + first[p][c] - gains[p] * image[p][c],) for c in range(3)
            ]
            for p in planes
        }
    wide = jnp.concatenate([v[p][c][0] for c in range(3) for p in (3, 4, 5)], axis=0)
    shape = (72, 144)
    to, source = iota(shape, 0), iota(shape, 1)
    left = (source // 16 == to // 8) & (source % 16 == 3 + to % 8 // 2)
    raised = exact_dot(exact_dot(left.astype(F32), wide), spread_matrix(wide.shape[1]))
    first, s, free, gains = mid_fields(mid)
    v = []
    for p in range(6):
        here = []
        for c in range(3):
            at = (c * 3 + p // 2) * 8
            here.append((first[p][c][0] + free[p] * raised[at : at + 8],))
        v.append(here)
    planes = range(1, 5)
    image = stencil(v, s, stiff_sums(s, planes), planes)
    wide = jnp.concatenate(
        [
            v[p][c][0] + first[p][c][0] - gains[p] * image[p][c]
            for c in range(3)
            for p in planes
        ],
        axis=0,
    )
    shape = (192, 96)
    to, source = iota(shape, 0), iota(shape, 1)
    inner = to % 16
    row = jnp.where(inner < 8, 2 + inner // 2, jnp.where(inner == 8, 6, 1))
    left = (source // 8 == to // 16) & (source % 8 == row)
    raised = exact_dot(exact_dot(left.astype(F32), wide), spread_matrix(wide.shape[1]))
    tiles = fine_tiles(fine, before, after, row_before, row_after)
    s = [t[3] for t in tiles]
    v = []
    for p in range(6):
        here = []
        for c in range(3):
            at = (c * 4 + (p + 1) // 2) * 16
            here.append(
                tuple(
                    tiles[p][c][k]
                    + tiles[p][4][k] * raised[at + 8 * k : at + 8 * k + 8]
                    for k in range(2)
                )
            )
        v.append(here)
    image = stencil(v, s, stiff_sums(s, planes), planes)
    for p in planes:
        g = gain(s[p][0], tiles[p][4][0])
        for c in range(3):
            out[c, p - 1] = v[p][c][0] + tiles[p][c][0] - g * image[p][c]


def call(kernel, shapes, *args):
    outs = [jax.ShapeDtypeStruct(shape, F32) for shape in shapes]
    return pl.pallas_call(
        kernel,
        out_shape=outs if len(outs) > 1 else outs[0],
        in_specs=[VMEM] * len(args),
        out_specs=[VMEM] * len(outs) if len(outs) > 1 else VMEM,
        compiler_params=PARAMS,
    )(*args)


def up(value, axis):
    n = lax.axis_size(axis)
    return lax.ppermute(value, axis, [(i, i + 1) for i in range(n - 1)])


def down(value, axis):
    n = lax.axis_size(axis)
    return lax.ppermute(value, axis, [(i + 1, i) for i in range(n - 1)])


def both_sides(low, high, axis):
    n = lax.axis_size(axis)
    even = lax.axis_index(axis) % 2 == 0
    inner = lax.ppermute(
        jnp.where(even, high, low), axis, [(i, i ^ 1) for i in range(n)]
    )
    outer = lax.ppermute(
        jnp.where(even, low, high),
        axis,
        [(i, ((i + 1) ^ 1) - 1) for i in range(1, n - 1)],
    )
    return jnp.where(even, outer, inner), jnp.where(even, inner, outer)


def gather_x(low):
    n = lax.axis_size("gx")
    groups = [[8 * g + i for i in range(8)] for g in range(n // 8)]
    row = lax.all_to_all(
        jnp.broadcast_to(low[None], (8,) + low.shape),
        "gx",
        0,
        0,
        axis_index_groups=groups,
    )
    place = lax.axis_index("gx") % 8
    first = place < 4
    moves = [(j, j + 8) for j in range(n - 8) if j % 8 < 4]
    moves += [(j, j - 8) for j in range(8, n) if j % 8 >= 4]
    other = lax.ppermute(jnp.where(first, row[4:], row[:4]), "gx", moves)
    planes = jnp.where(
        first, jnp.concatenate([other, row]), jnp.concatenate([row, other])
    )
    return lax.dynamic_slice_in_dim(planes, place % 4, 9, 0)


def per_device(density, fixed, loaded, load):
    nz = density.shape[2]
    fine, low_side, high_side = call(
        prepare_kernel,
        [(5, 4, 8, nz), (5, 8, nz), (5, 8, nz)],
        density,
        fixed,
        loaded,
        load,
    )
    before, after = both_sides(low_side, high_side, "gx")

    def edge(row):
        return jnp.concatenate(
            [before[:, None, row], fine[:, :, row], after[:, None, row]], axis=1
        )

    rims = (up(edge(7), "gy"), down(edge(0), "gy"))
    fine_args = (fine, before, after, *rims)
    mid = call(fine_residual_kernel, [(40, nz // 2)], *fine_args)

    sides = both_sides(mid, mid, "gx")
    shape = (5, 2, 4, nz // 2)
    mid = jnp.concatenate([a.reshape(shape) for a in (sides[0], mid, sides[1])], axis=1)
    rows_before = up(mid[:, :, 2:].reshape(60, nz // 2), "gy")
    rows_after = down(mid[:, :, :2].reshape(60, nz // 2), "gy")
    shape = (5, 6, 2, nz // 2)
    mid = jnp.concatenate(
        [rows_before.reshape(shape), mid, rows_after.reshape(shape)], axis=2
    )
    low = call(mid_residual_kernel, [(10, nz // 4)], mid)

    low = gather_x(low).reshape(90, nz // 4)
    near = up(low, "gy"), down(low, "gy")
    far = [up(near[0], "gy"), near[0], low, near[1], down(near[1], "gy")]
    low = jnp.stack(far).reshape(5, 9, 5, 2, nz // 4)
    low = low.transpose(2, 1, 0, 3, 4).reshape(5, 9, 10, nz // 4)
    low = jnp.pad(low, ((0, 0), (0, 0), (0, 6), (0, 0)))
    return call(finish_kernel, [(3, 4, 8, nz)], low, mid, *fine_args)


def solution(mesh):
    return jax.shard_map(
        per_device,
        mesh=mesh,
        in_specs=(
            P("gx", "gy", None),
            P("gx", "gy", None),
            P("gx", "gy", None),
            P(None, "gx", "gy", None),
        ),
        out_specs=P(None, "gx", "gy", None),
        check_vma=False,
    )
```

```python
import jax
import jax.numpy as jnp
from jax import lax
from jax.experimental import pallas as pl
from jax.experimental.pallas import tpu as pltpu
from jax.sharding import PartitionSpec as P

F32 = jnp.float32
VMEM = pl.BlockSpec(memory_space=pltpu.VMEM)
PARAMS = pltpu.CompilerParams(vmem_limit_bytes=48 * 1024 * 1024)


def iota(shape, dim):
    return lax.broadcasted_iota(jnp.int32, shape, dim)


def exact_dot(a, b):
    return jnp.dot(a, b, precision=lax.Precision.HIGHEST, preferred_element_type=F32)


def pool_matrix(n):
    shape = (n, n // 2)
    return (iota(shape, 0) // 2 == iota(shape, 1)).astype(F32)


def spread_matrix(n):
    shape = (n, 2 * n)
    return (iota(shape, 0) == iota(shape, 1) // 2).astype(F32)


def z_parts(tiles):
    t, d = [], []
    for a in tiles:
        n = a.shape[1]
        lane = iota(a.shape, 1)
        after = jnp.where(lane == n - 1, 0.0, pltpu.roll(a, n - 1, 1))
        before = jnp.where(lane == 0, 0.0, pltpu.roll(a, 1, 1))
        t.append((after + before) + 2.0 * a)
        d.append(after - before)
    return tuple(t), tuple(d)


def y_pair(tiles):
    a = tiles[0]
    n = a.shape[0]
    if len(tiles) == 1:
        return pltpu.roll(a, n - 1, 0), pltpu.roll(a, 1, 0)
    row = iota(a.shape, 0)
    after = pltpu.roll(jnp.where(row == 0, tiles[1], a), n - 1, 0)
    before = pltpu.roll(jnp.where(row == n - 1, tiles[1], a), 1, 0)
    return after, before


def y_t(tiles):
    after, before = y_pair(tiles)
    return (after + before) + 2.0 * tiles[0]


def y_d(tiles):
    after, before = y_pair(tiles)
    return after - before


def y_both(tiles):
    after, before = y_pair(tiles)
    return (after + before) + 2.0 * tiles[0], after - before


def plane_terms(v):
    (tx, dx), (ty, dy), (tz, dz) = [z_parts(c) for c in v]
    xt, xd = y_both(tx)
    xc = y_t(dx)
    yt, yd = y_both(ty)
    yc = y_d(dy)
    zt = y_t(tz)
    zb, zc = y_both(dz)
    return (
        (xt, yt + 0.25 * zc, zt + 0.25 * yc),
        (0.25 * (yd + zb), 0.25 * xd, 0.25 * xc),
    )


def scalar_terms(s):
    t, _ = z_parts(s)
    return y_t(t)


def times(a, b):
    return tuple(p * q for p, q in zip(a, b))


def stiff_sums(s, planes):
    terms = {p: scalar_terms(s[p]) for p in range(planes[0] - 1, planes[-1] + 2)}
    return {p: 2.0 * terms[p] + (terms[p + 1] + terms[p - 1]) for p in planes}


def stencil(v, s, sums, planes):
    own, scaled = {}, {}
    result = {}
    for p in range(planes[0] - 1, planes[-1] + 2):
        for store, field in ((own, v[p]), (scaled, [times(c, s[p]) for c in v[p]])):
            even, odd = plane_terms(field)
            store[p] = (
                [2.0 * e for e in even],
                [e + o for e, o in zip(even, odd)],
                [e - o for e, o in zip(even, odd)],
            )
        q = p - 1
        if q in planes:
            here = []
            for c in range(3):
                plain = own[q][0][c] + (own[q + 1][1][c] + own[q - 1][2][c])
                heavy = scaled[q][0][c] + (scaled[q + 1][1][c] + scaled[q - 1][2][c])
                u, k = v[q][c][0], s[q][0]
                here.append(8.1 * (k * u) + 0.125 * (u * sums[q] - (k * plain + heavy)))
            result[q] = here
    return result


def gain(stiff, free):
    return free * 0.8 / (7.1 * stiff + 7.5)


def prepare_kernel(density, fixed, loaded, load, fine, low_side, high_side, *scratch):
    copies = [
        pltpu.make_async_copy(source, scratch[k], scratch[4].at[k])
        for k, source in enumerate((density, fixed, loaded, load))
    ]
    for copy in copies:
        copy.start()
    for copy in copies:
        copy.wait()
    density, fixed, loaded, load = scratch[:4]
    for p in (0, 3, 1, 2):
        level = (density[p].astype(F32) + 1.0) * (1.0 / 256.0)
        stiff = 0.05 + level * level * level
        free = (1 - fixed[p]).astype(F32)
        factor = gain(stiff, free) * loaded[p].astype(F32)
        values = [factor * load[c, p] for c in range(3)] + [stiff, free]
        for f in range(5):
            fine[f, p] = values[f]
            if p == 0:
                low_side[f] = values[f]
            if p == 3:
                high_side[f] = values[f]


def fine_tiles(fine, before, after, row_before, row_after):
    row = iota((8, fine.shape[3]), 0)
    result = []
    for p in range(6):
        here = []
        for f in range(5):
            main = before[f] if p == 0 else after[f] if p == 5 else fine[f, p - 1]
            rim = jnp.where(
                row == 0, row_after[f, pl.ds(p, 1), :], row_before[f, pl.ds(p, 1), :]
            )
            here.append((main, rim))
        result.append(here)
    return result


def fine_residual_kernel(fine, before, after, row_before, row_after, mid):
    tiles = fine_tiles(fine, before, after, row_before, row_after)
    v = [t[:3] for t in tiles]
    s = [t[3] for t in tiles]
    planes = range(1, 5)
    image = stencil(v, s, stiff_sums(s, planes), planes)
    rows = [[], [], [], [], []]
    for p in planes:
        stiff, free = s[p][0], tiles[p][4][0]
        back = 1.25 * (7.1 * stiff + 7.5)
        for c in range(3):
            rows[c].append(free * (back * v[p][c][0] - image[p][c]))
        rows[3].append(stiff)
        rows[4].append(free)
    pairs = []
    for f in range(5):
        pairs += [rows[f][0] + rows[f][1], rows[f][2] + rows[f][3]]
    wide = jnp.concatenate(pairs, axis=0)
    short = exact_dot(wide, pool_matrix(wide.shape[1]))
    shape = (40, 80)
    left = (iota(shape, 0) == iota(shape, 1) // 2).astype(F32)
    sums = exact_dot(left, short)
    mid[0:24] = sums[0:24]
    mid[24:32] = sums[24:32] * 0.125
    mid[32:40] = (sums[32:40] > 0.5).astype(F32)


def mid_fields(mid):
    v, s, free, gains = [], [], [], []
    for p in range(6):
        stiff, open_ = mid[3, p], mid[4, p]
        g = gain(stiff, open_)
        v.append([(0.5 * g * mid[c, p],) for c in range(3)])
        s.append((stiff,))
        free.append(open_)
        gains.append(g)
    return v, s, free, gains


def mid_residual_kernel(mid, low):
    v, s, free, _ = mid_fields(mid)
    planes = range(2, 4)
    image = stencil(v, s, stiff_sums(s, planes), planes)
    pairs = []
    for c in range(3):
        pairs.append(
            sum(free[p] * (mid[c, p] - 2.0 * image[p][c]) for p in planes)
        )
    pairs.append(s[2][0] + s[3][0])
    pairs.append(free[2] + free[3])
    wide = jnp.concatenate(pairs, axis=0)
    short = exact_dot(wide, pool_matrix(wide.shape[1]))
    shape = (10, 40)
    out, source = iota(shape, 0), iota(shape, 1)
    left = (source // 8 == out // 2) & (source % 8 // 2 == 1 + out % 2)
    sums = exact_dot(left.astype(F32), short)
    row = iota(sums.shape, 0)
    values = jnp.where(
        row < 6, sums, jnp.where(row < 8, sums * 0.125, (sums > 0.5).astype(F32))
    )
    for k in range(low.shape[0]):
        low[k] = values


def finish_kernel(low, mid, fine, before, after, row_before, row_after, out):
    parts = [slice(0, 8), slice(8, 16)]
    s = [tuple(low[3, p, k] for k in parts) for p in range(9)]
    gains = [tuple(gain(low[3, p, k], low[4, p, k]) for k in parts) for p in range(9)]
    first = [
        [tuple(0.25 * gains[p][k] * low[c, p, parts[k]] for k in range(2)) for c in range(3)]
        for p in range(9)
    ]
    v = dict(enumerate(first))
    sums = stiff_sums(s, range(1, 8))
    for reach in (1, 2, 3):
        planes = range(reach, 9 - reach)
        image = stencil(v, s, sums, planes)
        v = {
            p: [
                (v[p][c][0] + first[p][c][0] - gains[p][0] * image[p][c],)
                for c in range(3)
            ]
            for p in planes
        }
    wide = jnp.concatenate([v[p][c][0] for c in range(3) for p in (3, 4, 5)], axis=0)
    shape = (72, 72)
    to, source = iota(shape, 0), iota(shape, 1)
    left = (source // 8 == to // 8) & (source % 8 == 2 + to % 8 // 2)
    raised = exact_dot(exact_dot(left.astype(F32), wide), spread_matrix(wide.shape[1]))
    first, s, free, gains = mid_fields(mid)
    v = []
    for p in range(6):
        here = []
        for c in range(3):
            at = (c * 3 + p // 2) * 8
            here.append((first[p][c][0] + free[p] * raised[at : at + 8],))
        v.append(here)
    planes = range(1, 5)
    image = stencil(v, s, stiff_sums(s, planes), planes)
    wide = jnp.concatenate(
        [
            v[p][c][0] + first[p][c][0] - gains[p] * image[p][c]
            for c in range(3)
            for p in planes
        ],
        axis=0,
    )
    shape = (192, 96)
    to, source = iota(shape, 0), iota(shape, 1)
    inner = to % 16
    row = jnp.where(inner < 8, 2 + inner // 2, jnp.where(inner == 8, 6, 1))
    left = (source // 8 == to // 16) & (source % 8 == row)
    raised = exact_dot(exact_dot(left.astype(F32), wide), spread_matrix(wide.shape[1]))
    tiles = fine_tiles(fine, before, after, row_before, row_after)
    s = [t[3] for t in tiles]
    v = []
    for p in range(6):
        here = []
        for c in range(3):
            at = (c * 4 + (p + 1) // 2) * 16
            here.append(
                tuple(
                    tiles[p][c][k]
                    + tiles[p][4][k] * raised[at + 8 * k : at + 8 * k + 8]
                    for k in range(2)
                )
            )
        v.append(here)
    image = stencil(v, s, stiff_sums(s, planes), planes)
    for p in planes:
        g = gain(s[p][0], tiles[p][4][0])
        for c in range(3):
            out[c, p - 1] = v[p][c][0] + tiles[p][c][0] - g * image[p][c]


def call(kernel, shapes, *args, space=pltpu.VMEM, scratch=()):
    outs = [jax.ShapeDtypeStruct(shape, F32) for shape in shapes]
    return pl.pallas_call(
        kernel,
        out_shape=outs if len(outs) > 1 else outs[0],
        in_specs=[pl.BlockSpec(memory_space=space)] * len(args),
        out_specs=[VMEM] * len(outs) if len(outs) > 1 else VMEM,
        scratch_shapes=list(scratch),
        compiler_params=PARAMS,
    )(*args)


def inner_swap(value, axis):
    return lax.ppermute(value, axis, [(i, i ^ 1) for i in range(lax.axis_size(axis))])


def outer_swap(value, axis):
    n = lax.axis_size(axis)
    return lax.ppermute(
        value, axis, [(i, ((i + 1) ^ 1) - 1) for i in range(1, n - 1)]
    )


def both_sides(low, high, axis):
    even = lax.axis_index(axis) % 2 == 0
    outer = outer_swap(jnp.where(even, low, high), axis)
    inner = inner_swap(jnp.where(even, high, low), axis)
    return jnp.where(even, outer, inner), jnp.where(even, inner, outer)


def gather_low(low):
    nx, ny = lax.axis_size("gx"), lax.axis_size("gy")
    nz = low.shape[2]
    groups = [
        [(8 * g + i) * ny + 2 * h + j for i in range(8) for j in range(2)]
        for g in range(nx // 8)
        for h in range(ny // 2)
    ]
    row = lax.all_to_all(low, ("gx", "gy"), 0, 0, axis_index_groups=groups)
    place = lax.axis_index("gx") % 8
    first = place < 4
    moves = [(j, j + 8) for j in range(nx - 8) if j % 8 < 4]
    moves += [(j, j - 8) for j in range(8, nx) if j % 8 >= 4]
    other = lax.ppermute(jnp.where(first, row[8:], row[:8]), "gx", moves)
    planes = jnp.where(
        first, jnp.concatenate([other, row]), jnp.concatenate([row, other])
    )
    pair = lax.dynamic_slice_in_dim(planes, place % 4 * 2, 18, 0)
    even = lax.axis_index("gy") % 2 == 0
    beside = outer_swap(pair.reshape(180, nz), "gy").reshape(9, 2, 10, nz)
    beyond = jnp.where(even, beside[:, 1], beside[:, 0]).reshape(90, nz)
    beyond = inner_swap(beyond, "gy").reshape(9, 1, 10, nz)
    pair = pair.reshape(9, 2, 10, nz)
    return jnp.where(
        even,
        jnp.concatenate([beside, pair, beyond], axis=1),
        jnp.concatenate([beyond, pair, beside], axis=1),
    )


def per_device(density, fixed, loaded, load):
    nz = density.shape[2]
    args = (density, fixed, loaded, load)
    fine, low_side, high_side = call(
        prepare_kernel,
        [(5, 4, 8, nz), (5, 8, nz), (5, 8, nz)],
        *args,
        space=pl.ANY,
        scratch=[pltpu.VMEM(a.shape, a.dtype) for a in args]
        + [pltpu.SemaphoreType.DMA((4,))],
    )
    before, after = both_sides(low_side, high_side, "gx")

    def edge(row):
        planes = [before[:, None, row], fine[:, :, row], after[:, None, row]]
        return jnp.concatenate(planes, axis=1).reshape(30, nz)

    rims = [r.reshape(5, 6, nz) for r in both_sides(edge(0), edge(7), "gy")]
    fine_args = (fine, before, after, *rims)
    mid = call(fine_residual_kernel, [(40, nz // 2)], *fine_args)

    sides = both_sides(mid, mid, "gx")
    shape = (5, 2, 4, nz // 2)
    mid = jnp.concatenate([a.reshape(shape) for a in (sides[0], mid, sides[1])], axis=1)
    rows_before, rows_after = both_sides(
        mid[:, :, :2].reshape(60, nz // 2), mid[:, :, 2:].reshape(60, nz // 2), "gy"
    )
    shape = (5, 6, 2, nz // 2)
    mid = jnp.concatenate(
        [rows_before.reshape(shape), mid, rows_after.reshape(shape)], axis=2
    )
    low = call(mid_residual_kernel, [(16, 10, nz // 4)], mid)
    low = gather_low(low).reshape(9, 5, 5, 2, nz // 4)
    low = low.transpose(2, 0, 1, 3, 4).reshape(5, 9, 10, nz // 4)
    low = jnp.concatenate(
        [low[:, :, 1:], jnp.zeros((5, 9, 6, nz // 4), F32), low[:, :, :1]], axis=2
    )
    return call(finish_kernel, [(3, 4, 8, nz)], low, mid, *fine_args)


def solution(mesh):
    return jax.shard_map(
        per_device,
        mesh=mesh,
        in_specs=(
            P("gx", "gy", None),
            P("gx", "gy", None),
            P("gx", "gy", None),
            P(None, "gx", "gy", None),
        ),
        out_specs=P(None, "gx", "gy", None),
        check_vma=False,
    )
```

```python
import jax
import jax.numpy as jnp
from jax import lax
from jax.experimental import pallas as pl
from jax.experimental.pallas import tpu as pltpu
from jax.sharding import PartitionSpec as P

F32 = jnp.float32
EXTRA = 8
HBM = pl.BlockSpec(memory_space=pltpu.HBM)
SMEM = pl.BlockSpec(memory_space=pltpu.SMEM)
VMEM = pl.BlockSpec(memory_space=pltpu.VMEM)
PARAMS = pltpu.CompilerParams(vmem_limit_bytes=48 * 1024 * 1024)


def iota(shape, dim):
    return lax.broadcasted_iota(jnp.int32, shape, dim)


def pick_rows(a, index):
    return jnp.take_along_axis(a, index, axis=0)


def lanes(a, k):
    return a[:, 128 * k : 128 * (k + 1)]


def spread_lanes(a):
    half = iota((8, 128), 1) // 2
    tiles = []
    for k in range(a.shape[1] // 128):
        for index in (half, half + 64):
            tiles.append(jnp.take_along_axis(lanes(a, k), index, axis=1))
    return jnp.concatenate(tiles, axis=1)


def pool_lanes(a):
    a = a + pltpu.roll(a, a.shape[1] - 1, 1)
    lane = iota((8, 128), 1)
    index = lane % 64 * 2
    tiles = []
    for k in range(0, a.shape[1] // 128, 2):
        low = jnp.take_along_axis(lanes(a, k), index, axis=1)
        high = jnp.take_along_axis(lanes(a, k + 1), index, axis=1)
        tiles.append(jnp.where(lane < 64, low, high))
    return jnp.concatenate(tiles, axis=1)


def z_parts(tiles):
    t, d = [], []
    for a in tiles:
        n = a.shape[1]
        lane = iota(a.shape, 1)
        after = jnp.where(lane == n - 1, 0.0, pltpu.roll(a, n - 1, 1))
        before = jnp.where(lane == 0, 0.0, pltpu.roll(a, 1, 1))
        t.append((after + before) + 2.0 * a)
        d.append(after - before)
    return tuple(t), tuple(d)


def y_pair(tiles):
    a = tiles[0]
    n = a.shape[0]
    if len(tiles) == 1:
        return pltpu.roll(a, n - 1, 0), pltpu.roll(a, 1, 0)
    row = iota(a.shape, 0)
    after = pltpu.roll(jnp.where(row == 0, tiles[1], a), n - 1, 0)
    before = pltpu.roll(jnp.where(row == n - 1, tiles[1], a), 1, 0)
    return after, before


def y_t(tiles):
    after, before = y_pair(tiles)
    return (after + before) + 2.0 * tiles[0]


def y_d(tiles):
    after, before = y_pair(tiles)
    return after - before


def y_both(tiles):
    after, before = y_pair(tiles)
    return (after + before) + 2.0 * tiles[0], after - before


def plane_terms(v):
    (tx, dx), (ty, dy), (tz, dz) = [z_parts(c) for c in v]
    xt, xd = y_both(tx)
    xc = y_t(dx)
    yt, yd = y_both(ty)
    yc = y_d(dy)
    zt = y_t(tz)
    zb, zc = y_both(dz)
    return (
        (xt, yt + 0.25 * zc, zt + 0.25 * yc),
        (0.25 * (yd + zb), 0.25 * xd, 0.25 * xc),
    )


def scalar_terms(s):
    t, _ = z_parts(s)
    return y_t(t)


def times(a, b):
    return tuple(p * q for p, q in zip(a, b))


def stiff_sums(s, planes):
    terms = {p: scalar_terms(s[p]) for p in range(planes[0] - 1, planes[-1] + 2)}
    return {p: 2.0 * terms[p] + (terms[p + 1] + terms[p - 1]) for p in planes}


def stencil(v, s, sums, planes, use=None):
    own, scaled = {}, {}
    result = {}
    for p in range(planes[0] - 1, planes[-1] + 2):
        for store, field in ((own, v[p]), (scaled, [times(c, s[p]) for c in v[p]])):
            even, odd = plane_terms(field)
            store[p] = (
                [2.0 * e for e in even],
                [e + o for e, o in zip(even, odd)],
                [e - o for e, o in zip(even, odd)],
            )
        q = p - 1
        if q in planes:
            here = []
            for c in range(3):
                plain = own[q][0][c] + (own[q + 1][1][c] + own[q - 1][2][c])
                heavy = scaled[q][0][c] + (scaled[q + 1][1][c] + scaled[q - 1][2][c])
                u, k = v[q][c][0], s[q][0]
                here.append(8.1 * (k * u) + 0.125 * (u * sums[q] - (k * plain + heavy)))
            result[q] = here
            if use is not None:
                use(q, here)
    return result


def gain(stiff, free):
    return free * 0.8 / (7.1 * stiff + 7.5)


def run_copies(pairs, sems):
    copies = [
        pltpu.make_async_copy(source, target, sems.at[k])
        for k, (source, target) in enumerate(pairs)
    ]
    for copy in copies:
        copy.start()
    for copy in copies:
        copy.wait()


def start_values(density, fixed, loaded, load):
    level = (density.astype(F32) + 1.0) * (1.0 / 256.0)
    stiff = 0.05 + level * level * level
    free = (1 - fixed).astype(F32)
    factor = gain(stiff, free) * loaded.astype(F32)
    return [factor * c for c in load] + [stiff, free]


def edge_kernel(even, density, fixed, loaded, load, outer, *scratch):
    plane = jnp.where(even[0] == 1, 0, 3)
    sources = [a.at[plane] for a in (density, fixed, loaded)] + [load.at[:, plane]]
    run_copies(zip(sources, scratch[:4]), scratch[4])
    d, x, m, f = scratch[:4]
    values = start_values(d[...], x[...], m[...], [f[c] for c in range(3)])
    for k in range(5):
        outer[k] = values[k]


def prepare_kernel(even, density, fixed, loaded, load, fine, inner, *scratch):
    run_copies(zip((density, fixed, loaded, load), scratch[:4]), scratch[4])
    d, x, m, f = scratch[:4]
    is_even = even[0] == 1
    kept = {}
    for p in range(4):
        values = start_values(d[p], x[p], m[p], [f[c, p] for c in range(3)])
        for k in range(5):
            fine[k, p] = values[k]
        kept[p] = values
    for k in range(5):
        inner[k] = jnp.where(is_even, kept[3][k], kept[0][k])


def fine_tiles(fine, before, after, row_before, row_after):
    row = iota((8, fine.shape[3]), 0)
    result = []
    for p in range(6):
        here = []
        for f in range(5):
            main = before[f] if p == 0 else after[f] if p == 5 else fine[f, p - 1]
            rim = jnp.where(
                row == 0, row_after[f, pl.ds(p, 1), :], row_before[f, pl.ds(p, 1), :]
            )
            here.append((main, rim))
        result.append(here)
    return result


def fine_residual_kernel(fine, before, after, row_before, row_after, mid):
    tiles = fine_tiles(fine, before, after, row_before, row_after)
    v = [t[:3] for t in tiles]
    s = [t[3] for t in tiles]
    planes = range(1, 5)
    image = stencil(v, s, stiff_sums(s, planes), planes)
    rows = [[], [], [], [], []]
    for p in planes:
        stiff, free = s[p][0], tiles[p][4][0]
        back = 1.25 * (7.1 * stiff + 7.5)
        for c in range(3):
            rows[c].append(free * (back * v[p][c][0] - image[p][c]))
        rows[3].append(stiff)
        rows[4].append(free)
    row = iota((8, rows[0][0].shape[1]), 0)
    index = row % 4 * 2
    for f in range(5):
        halves = []
        for x in (0, 2):
            both = rows[f][x] + rows[f][x + 1]
            halves.append(pick_rows(both + pltpu.roll(both, 7, 0), index))
        total = pool_lanes(jnp.where(row < 4, halves[0], halves[1]))
        if f == 3:
            total = total * 0.125
        if f == 4:
            total = (total > 0.5).astype(F32)
        mid[8 * f : 8 * f + 8] = total


def mid_fields(mid):
    v, s, free, gains = [], [], [], []
    for p in range(6):
        stiff, open_ = mid[3, p], mid[4, p]
        g = gain(stiff, open_)
        v.append([(0.5 * g * mid[c, p],) for c in range(3)])
        s.append((stiff,))
        free.append(open_)
        gains.append(g)
    return v, s, free, gains


def mid_residual_kernel(mid, low):
    v, s, free, _ = mid_fields(mid)
    planes = range(2, 4)
    image = stencil(v, s, stiff_sums(s, planes), planes)
    pairs = []
    for c in range(3):
        pairs.append(
            sum(free[p] * (mid[c, p] - 2.0 * image[p][c]) for p in planes)
        )
    pairs.append(s[2][0] + s[3][0])
    pairs.append(free[2] + free[3])
    sums = [pool_lanes(a + pltpu.roll(a, 7, 0)) for a in pairs]
    sums[3] = sums[3] * 0.125
    sums[4] = (sums[4] > 0.5).astype(F32)
    row = iota(sums[0].shape, 0)
    index = 2 + row % 2 * 2
    packed = pick_rows(sums[0], index)
    for f in range(1, 4):
        packed = jnp.where(row // 2 == f, pick_rows(sums[f], index), packed)
    last = pick_rows(sums[4], index)[0:2]
    for k in range(low.shape[0]):
        low[k, 0:8] = packed
        low[k, 8:10] = last


def finish_kernel(
    low, mid, fine, before, after, row_before, row_after, out, held, sems
):
    parts = [slice(0, 8), slice(8, 16)]
    s = [tuple(low[3, p, k] for k in parts) for p in range(9)]
    gains = [tuple(gain(low[3, p, k], low[4, p, k]) for k in parts) for p in range(9)]
    first = [
        [tuple(0.25 * gains[p][k] * low[c, p, parts[k]] for k in range(2)) for c in range(3)]
        for p in range(9)
    ]
    v = dict(enumerate(first))
    sums = stiff_sums(s, range(1, 8))
    for reach in (1, 2, 3):
        planes = range(reach, 9 - reach)
        image = stencil(v, s, sums, planes)
        v = {
            p: [
                (v[p][c][0] + first[p][c][0] - gains[p][0] * image[p][c],)
                for c in range(3)
            ]
            for p in planes
        }
    row = iota((8, low.shape[3]), 0)
    raised = [
        [spread_lanes(pick_rows(v[p][c][0], 2 + row // 2)) for p in (3, 4, 5)]
        for c in range(3)
    ]
    first, s, free, gains = mid_fields(mid)
    v = []
    for p in range(6):
        here = []
        for c in range(3):
            here.append((first[p][c][0] + free[p] * raised[c][p // 2],))
        v.append(here)
    planes = range(1, 5)
    image = stencil(v, s, stiff_sums(s, planes), planes)
    row = iota((8, mid.shape[3]), 0)
    picks = (2 + row // 2, jnp.where(row == 0, 6, 1))
    raised = []
    for c in range(3):
        raised.append([])
        for p in planes:
            a = v[p][c][0] + first[p][c][0] - gains[p] * image[p][c]
            raised[c].append([spread_lanes(pick_rows(a, index)) for index in picks])
    tiles = fine_tiles(fine, before, after, row_before, row_after)
    s = [t[3] for t in tiles]
    v = []
    for p in range(6):
        here = []
        for c in range(3):
            up = raised[c][(p + 1) // 2]
            here.append(
                tuple(tiles[p][c][k] + tiles[p][4][k] * up[k] for k in range(2))
            )
        v.append(here)
    sums = stiff_sums(s, planes)
    copies = []

    def finish(p, image):
        g = gain(s[p][0], tiles[p][4][0])
        for c in range(3):
            held[c, p - 1] = v[p][c][0] + tiles[p][c][0] - g * image[c]
        copies.append(
            pltpu.make_async_copy(held.at[:, p - 1], out.at[:, p - 1], sems.at[p - 1])
        )
        copies[-1].start()

    stencil(v, s, sums, planes, finish)
    for copy in copies:
        copy.wait()


def call(kernel, shapes, *args, ins=None, outs=None, scratch=()):
    results = [jax.ShapeDtypeStruct(shape, F32) for shape in shapes]
    outs = outs or [VMEM] * len(results)
    return pl.pallas_call(
        kernel,
        out_shape=results if len(results) > 1 else results[0],
        in_specs=ins or [VMEM] * len(args),
        out_specs=outs if len(results) > 1 else outs[0],
        scratch_shapes=list(scratch),
        compiler_params=PARAMS,
    )(*args)


def inner_swap(value, axis):
    return lax.ppermute(value, axis, [(i, i ^ 1) for i in range(lax.axis_size(axis))])


def outer_swap(value, axis):
    n = lax.axis_size(axis)
    return lax.ppermute(
        value, axis, [(i, ((i + 1) ^ 1) - 1) for i in range(1, n - 1)]
    )


def both_sides(low, high, axis):
    even = lax.axis_index(axis) % 2 == 0
    wide = jnp.where(even, low, high)
    rows = low.shape[0]
    outer = outer_swap(jnp.concatenate([wide, wide[:EXTRA]]), axis)[:rows]
    inner = inner_swap(jnp.where(even, high, low), axis)
    return jnp.where(even, outer, inner), jnp.where(even, inner, outer)


def gather_low(low):
    nx, ny = lax.axis_size("gx"), lax.axis_size("gy")
    nz = low.shape[2]
    groups = [
        [(8 * g + i) * ny + 2 * h + j for i in range(8) for j in range(2)]
        for g in range(nx // 8)
        for h in range(ny // 2)
    ]
    row = lax.all_to_all(low, ("gx", "gy"), 0, 0, axis_index_groups=groups)
    place = lax.axis_index("gx") % 8
    first = place < 4
    moves = [(j, j + 8) for j in range(nx - 8) if j % 8 < 4]
    moves += [(j, j - 8) for j in range(8, nx) if j % 8 >= 4]
    other = lax.ppermute(jnp.where(first, row[8:], row[:8]), "gx", moves)
    planes = jnp.where(
        first, jnp.concatenate([other, row]), jnp.concatenate([row, other])
    )
    pair = lax.dynamic_slice_in_dim(planes, place % 4 * 2, 18, 0)
    even = lax.axis_index("gy") % 2 == 0
    beside = outer_swap(pair.reshape(180, nz), "gy").reshape(9, 2, 10, nz)
    beyond = jnp.where(even, beside[:, 1], beside[:, 0]).reshape(90, nz)
    beyond = inner_swap(beyond, "gy").reshape(9, 1, 10, nz)
    pair = pair.reshape(9, 2, 10, nz)
    return jnp.where(
        even,
        jnp.concatenate([beside, pair, beyond], axis=1),
        jnp.concatenate([beyond, pair, beside], axis=1),
    )


def per_device(density, fixed, loaded, load):
    nz = density.shape[2]
    even = lax.axis_index("gx") % 2 == 0
    args = (even.astype(jnp.int32).reshape(1), density, fixed, loaded, load)
    ins = [SMEM] + [HBM] * 4
    sems = pltpu.SemaphoreType.DMA((4,))
    outer = call(
        edge_kernel,
        [(5, 8, nz)],
        *args,
        ins=ins,
        scratch=[pltpu.VMEM((8, nz), a.dtype) for a in args[1:4]]
        + [pltpu.VMEM((3, 8, nz), F32), sems],
    )
    outer = outer_swap(outer, "gx")
    fine, inner = call(
        prepare_kernel,
        [(5, 4, 8, nz), (5, 8, nz)],
        *args,
        ins=ins,
        scratch=[pltpu.VMEM(a.shape, a.dtype) for a in args[1:]] + [sems],
    )
    inner = inner_swap(inner, "gx")
    before, after = jnp.where(even, outer, inner), jnp.where(even, inner, outer)

    def edge(row):
        planes = [before[:, None, row], fine[:, :, row], after[:, None, row]]
        return jnp.concatenate(planes, axis=1).reshape(30, nz)

    rims = [r.reshape(5, 6, nz) for r in both_sides(edge(0), edge(7), "gy")]
    fine_args = (fine, before, after, *rims)
    mid = call(fine_residual_kernel, [(40, nz // 2)], *fine_args)

    sides = both_sides(mid, mid, "gx")
    shape = (5, 2, 4, nz // 2)
    mid = jnp.concatenate([a.reshape(shape) for a in (sides[0], mid, sides[1])], axis=1)
    rows_before, rows_after = both_sides(
        mid[:, :, :2].reshape(60, nz // 2), mid[:, :, 2:].reshape(60, nz // 2), "gy"
    )
    shape = (5, 6, 2, nz // 2)
    mid = jnp.concatenate(
        [rows_before.reshape(shape), mid, rows_after.reshape(shape)], axis=2
    )
    low = call(mid_residual_kernel, [(16, 10, nz // 4)], mid)
    low = gather_low(low).reshape(9, 5, 5, 2, nz // 4)
    low = low.transpose(2, 0, 1, 3, 4).reshape(5, 9, 10, nz // 4)
    low = jnp.concatenate(
        [low[:, :, 1:], jnp.zeros((5, 9, 6, nz // 4), F32), low[:, :, :1]], axis=2
    )
    return call(
        finish_kernel,
        [(3, 4, 8, nz)],
        low,
        mid,
        *fine_args,
        outs=[HBM],
        scratch=[pltpu.VMEM((3, 4, 8, nz), F32), sems],
    )


def solution(mesh):
    return jax.shard_map(
        per_device,
        mesh=mesh,
        in_specs=(
            P("gx", "gy", None),
            P("gx", "gy", None),
            P("gx", "gy", None),
            P(None, "gx", "gy", None),
        ),
        out_specs=P(None, "gx", "gy", None),
        check_vma=False,
    )
```

```python
import jax
import jax.numpy as jnp
from jax import lax
from jax.experimental import pallas as pl
from jax.experimental.pallas import tpu as pltpu
from jax.sharding import PartitionSpec as P

F32 = jnp.float32
EXTRA = 8
HBM = pl.BlockSpec(memory_space=pltpu.HBM)
SMEM = pl.BlockSpec(memory_space=pltpu.SMEM)
VMEM = pl.BlockSpec(memory_space=pltpu.VMEM)


def iota(shape, dim):
    return lax.broadcasted_iota(jnp.int32, shape, dim)


def pick_rows(a, index):
    return jnp.take_along_axis(a, index, axis=0)


def lanes(a, k):
    return a[:, 128 * k : 128 * (k + 1)]


def spread_lanes(a):
    half = iota((8, 128), 1) // 2
    tiles = []
    for k in range(a.shape[1] // 128):
        for index in (half, half + 64):
            tiles.append(jnp.take_along_axis(lanes(a, k), index, axis=1))
    return jnp.concatenate(tiles, axis=1)


def pool_lanes(a):
    a = a + pltpu.roll(a, a.shape[1] - 1, 1)
    lane = iota((8, 128), 1)
    index = lane % 64 * 2
    tiles = []
    for k in range(0, a.shape[1] // 128, 2):
        low = jnp.take_along_axis(lanes(a, k), index, axis=1)
        high = jnp.take_along_axis(lanes(a, k + 1), index, axis=1)
        tiles.append(jnp.where(lane < 64, low, high))
    return jnp.concatenate(tiles, axis=1)


def z_parts(tiles):
    t, d = [], []
    for a in tiles:
        n = a.shape[1]
        lane = iota(a.shape, 1)
        after = jnp.where(lane == n - 1, 0.0, pltpu.roll(a, n - 1, 1))
        before = jnp.where(lane == 0, 0.0, pltpu.roll(a, 1, 1))
        t.append((after + before) + 2.0 * a)
        d.append(after - before)
    return tuple(t), tuple(d)


def y_pair(tiles):
    a = tiles[0]
    n = a.shape[0]
    if len(tiles) == 1:
        return pltpu.roll(a, n - 1, 0), pltpu.roll(a, 1, 0)
    row = iota(a.shape, 0)
    after = pltpu.roll(jnp.where(row == 0, tiles[1], a), n - 1, 0)
    before = pltpu.roll(jnp.where(row == n - 1, tiles[1], a), 1, 0)
    return after, before


def y_t(tiles):
    after, before = y_pair(tiles)
    return (after + before) + 2.0 * tiles[0]


def y_d(tiles):
    after, before = y_pair(tiles)
    return after - before


def y_both(tiles):
    after, before = y_pair(tiles)
    return (after + before) + 2.0 * tiles[0], after - before


def plane_terms(v):
    (tx, dx), (ty, dy), (tz, dz) = [z_parts(c) for c in v]
    xt, xd = y_both(tx)
    xc = y_t(dx)
    yt, yd = y_both(ty)
    yc = y_d(dy)
    zt = y_t(tz)
    zb, zc = y_both(dz)
    return (
        (xt, yt + 0.25 * zc, zt + 0.25 * yc),
        (0.25 * (yd + zb), 0.25 * xd, 0.25 * xc),
    )


def scalar_terms(s):
    t, _ = z_parts(s)
    return y_t(t)


def times(a, b):
    return tuple(p * q for p, q in zip(a, b))


def stiff_sums(s, planes):
    terms = {p: scalar_terms(s[p]) for p in range(planes[0] - 1, planes[-1] + 2)}
    return {p: 2.0 * terms[p] + (terms[p + 1] + terms[p - 1]) for p in planes}


def stencil(v, s, sums, planes, use=None):
    own, scaled = {}, {}
    result = {}
    for p in range(planes[0] - 1, planes[-1] + 2):
        for store, field in ((own, v[p]), (scaled, [times(c, s[p]) for c in v[p]])):
            even, odd = plane_terms(field)
            store[p] = (
                [2.0 * e for e in even],
                [e + o for e, o in zip(even, odd)],
                [e - o for e, o in zip(even, odd)],
            )
        q = p - 1
        if q in planes:
            here = []
            for c in range(3):
                plain = own[q][0][c] + (own[q + 1][1][c] + own[q - 1][2][c])
                heavy = scaled[q][0][c] + (scaled[q + 1][1][c] + scaled[q - 1][2][c])
                u, k = v[q][c][0], s[q][0]
                here.append(8.1 * (k * u) + 0.125 * (u * sums[q] - (k * plain + heavy)))
            result[q] = here
            if use is not None:
                use(q, here)
    return result


def gain(stiff, free):
    return free * 0.8 / (7.1 * stiff + 7.5)


def run_copies(pairs, sems):
    copies = [
        pltpu.make_async_copy(source, target, sems.at[k])
        for k, (source, target) in enumerate(pairs)
    ]
    for copy in copies:
        copy.start()
    for copy in copies:
        copy.wait()


def start_values(density, fixed, loaded, load):
    level = (density.astype(F32) + 1.0) * (1.0 / 256.0)
    stiff = 0.05 + level * level * level
    free = (1 - fixed).astype(F32)
    factor = gain(stiff, free) * loaded.astype(F32)
    return [factor * c for c in load] + [stiff, free]


def edge_kernel(even, density, fixed, loaded, load, outer, *scratch):
    plane = jnp.where(even[0] == 1, 0, 3)
    sources = [a.at[plane] for a in (density, fixed, loaded)] + [load.at[:, plane]]
    run_copies(zip(sources, scratch[:4]), scratch[4])
    d, x, m, f = scratch[:4]
    values = start_values(d[...], x[...], m[...], [f[c] for c in range(3)])
    for k in range(5):
        outer[k] = values[k]


def prepare_kernel(even, density, fixed, loaded, load, fine, inner, *scratch):
    run_copies(zip((density, fixed, loaded, load), scratch[:4]), scratch[4])
    d, x, m, f = scratch[:4]
    is_even = even[0] == 1
    kept = {}
    for p in range(4):
        values = start_values(d[p], x[p], m[p], [f[c, p] for c in range(3)])
        for k in range(5):
            fine[k, p] = values[k]
        kept[p] = values
    for k in range(5):
        inner[k] = jnp.where(is_even, kept[3][k], kept[0][k])


def fine_tiles(fine, before, after, row_before, row_after):
    row = iota((8, fine.shape[3]), 0)
    result = []
    for p in range(6):
        here = []
        for f in range(5):
            main = before[f] if p == 0 else after[f] if p == 5 else fine[f, p - 1]
            rim = jnp.where(
                row == 0, row_after[f, pl.ds(p, 1), :], row_before[f, pl.ds(p, 1), :]
            )
            here.append((main, rim))
        result.append(here)
    return result


def fine_residual_kernel(fine, before, after, row_before, row_after, mid):
    tiles = fine_tiles(fine, before, after, row_before, row_after)
    v = [t[:3] for t in tiles]
    s = [t[3] for t in tiles]
    planes = range(1, 5)
    image = stencil(v, s, stiff_sums(s, planes), planes)
    rows = [[], [], [], [], []]
    for p in planes:
        stiff, free = s[p][0], tiles[p][4][0]
        back = 1.25 * (7.1 * stiff + 7.5)
        for c in range(3):
            rows[c].append(free * (back * v[p][c][0] - image[p][c]))
        rows[3].append(stiff)
        rows[4].append(free)
    row = iota((8, rows[0][0].shape[1]), 0)
    index = row % 4 * 2
    for f in range(5):
        halves = []
        for x in (0, 2):
            both = rows[f][x] + rows[f][x + 1]
            halves.append(pick_rows(both + pltpu.roll(both, 7, 0), index))
        total = pool_lanes(jnp.where(row < 4, halves[0], halves[1]))
        if f == 3:
            total = total * 0.125
        if f == 4:
            total = (total > 0.5).astype(F32)
        mid[8 * f : 8 * f + 8] = total


def mid_fields(mid):
    v, s, free, gains = [], [], [], []
    for p in range(6):
        stiff, open_ = mid[3, p], mid[4, p]
        g = gain(stiff, open_)
        v.append([(0.5 * g * mid[c, p],) for c in range(3)])
        s.append((stiff,))
        free.append(open_)
        gains.append(g)
    return v, s, free, gains


def mid_residual_kernel(mid, low):
    v, s, free, _ = mid_fields(mid)
    planes = range(2, 4)
    image = stencil(v, s, stiff_sums(s, planes), planes)
    pairs = []
    for c in range(3):
        pairs.append(
            sum(free[p] * (mid[c, p] - 2.0 * image[p][c]) for p in planes)
        )
    pairs.append(s[2][0] + s[3][0])
    pairs.append(free[2] + free[3])
    sums = [pool_lanes(a + pltpu.roll(a, 7, 0)) for a in pairs]
    sums[3] = sums[3] * 0.125
    sums[4] = (sums[4] > 0.5).astype(F32)
    row = iota(sums[0].shape, 0)
    index = 2 + row % 2 * 2
    packed = pick_rows(sums[0], index)
    for f in range(1, 4):
        packed = jnp.where(row // 2 == f, pick_rows(sums[f], index), packed)
    last = pick_rows(sums[4], index)[0:2]
    for k in range(low.shape[0]):
        low[k, 0:8] = packed
        low[k, 8:10] = last


def finish_kernel(
    low, mid, fine, before, after, row_before, row_after, out, held, sems
):
    parts = [slice(0, 8), slice(8, 16)]
    s = [tuple(low[3, p, k] for k in parts) for p in range(9)]
    gains = [tuple(gain(low[3, p, k], low[4, p, k]) for k in parts) for p in range(9)]
    first = [
        [tuple(0.25 * gains[p][k] * low[c, p, parts[k]] for k in range(2)) for c in range(3)]
        for p in range(9)
    ]
    v = dict(enumerate(first))
    sums = stiff_sums(s, range(1, 8))
    for reach in (1, 2, 3):
        planes = range(reach, 9 - reach)
        image = stencil(v, s, sums, planes)
        v = {
            p: [
                (v[p][c][0] + first[p][c][0] - gains[p][0] * image[p][c],)
                for c in range(3)
            ]
            for p in planes
        }
    row = iota((8, low.shape[3]), 0)
    raised = [
        [spread_lanes(pick_rows(v[p][c][0], 2 + row // 2)) for p in (3, 4, 5)]
        for c in range(3)
    ]
    first, s, free, gains = mid_fields(mid)
    v = []
    for p in range(6):
        here = []
        for c in range(3):
            here.append((first[p][c][0] + free[p] * raised[c][p // 2],))
        v.append(here)
    planes = range(1, 5)
    image = stencil(v, s, stiff_sums(s, planes), planes)
    row = iota((8, mid.shape[3]), 0)
    picks = (2 + row // 2, jnp.where(row == 0, 6, 1))
    raised = []
    for c in range(3):
        raised.append([])
        for p in planes:
            a = v[p][c][0] + first[p][c][0] - gains[p] * image[p][c]
            raised[c].append([spread_lanes(pick_rows(a, index)) for index in picks])
    tiles = fine_tiles(fine, before, after, row_before, row_after)
    s = [t[3] for t in tiles]
    v = []
    for p in range(6):
        here = []
        for c in range(3):
            up = raised[c][(p + 1) // 2]
            here.append(
                tuple(tiles[p][c][k] + tiles[p][4][k] * up[k] for k in range(2))
            )
        v.append(here)
    sums = stiff_sums(s, planes)
    copies = []

    def finish(p, image):
        g = gain(s[p][0], tiles[p][4][0])
        for c in range(3):
            held[c, p - 1] = v[p][c][0] + tiles[p][c][0] - g * image[c]
        copies.append(
            pltpu.make_async_copy(held.at[:, p - 1], out.at[:, p - 1], sems.at[p - 1])
        )
        copies[-1].start()

    stencil(v, s, sums, planes, finish)
    for copy in copies:
        copy.wait()


def call(kernel, shapes, *args, ins=None, outs=None, scratch=(), limit=48):
    results = [jax.ShapeDtypeStruct(shape, F32) for shape in shapes]
    outs = outs or [VMEM] * len(results)
    return pl.pallas_call(
        kernel,
        out_shape=results if len(results) > 1 else results[0],
        in_specs=ins or [VMEM] * len(args),
        out_specs=outs if len(results) > 1 else outs[0],
        scratch_shapes=list(scratch),
        compiler_params=pltpu.CompilerParams(vmem_limit_bytes=limit << 20),
    )(*args)


def inner_swap(value, axis):
    return lax.ppermute(value, axis, [(i, i ^ 1) for i in range(lax.axis_size(axis))])


def outer_swap(value, axis):
    n = lax.axis_size(axis)
    return lax.ppermute(
        value, axis, [(i, ((i + 1) ^ 1) - 1) for i in range(1, n - 1)]
    )


def both_sides(low, high, axis):
    even = lax.axis_index(axis) % 2 == 0
    wide = jnp.where(even, low, high)
    rows = low.shape[0]
    outer = outer_swap(jnp.concatenate([wide, wide[:EXTRA]]), axis)[:rows]
    inner = inner_swap(jnp.where(even, high, low), axis)
    return jnp.where(even, outer, inner), jnp.where(even, inner, outer)


def gather_low(low):
    nx, ny = lax.axis_size("gx"), lax.axis_size("gy")
    nz = low.shape[2]
    groups = [
        [(8 * g + i) * ny + 2 * h + j for i in range(8) for j in range(2)]
        for g in range(nx // 8)
        for h in range(ny // 2)
    ]
    row = lax.all_to_all(low, ("gx", "gy"), 0, 0, axis_index_groups=groups)
    place = lax.axis_index("gx") % 8
    first = place < 4
    moves = [(j, j + 8) for j in range(nx - 8) if j % 8 < 4]
    moves += [(j, j - 8) for j in range(8, nx) if j % 8 >= 4]
    other = lax.ppermute(jnp.where(first, row[8:], row[:8]), "gx", moves)
    planes = jnp.where(
        first, jnp.concatenate([other, row]), jnp.concatenate([row, other])
    )
    pair = lax.dynamic_slice_in_dim(planes, place % 4 * 2, 18, 0)
    even = lax.axis_index("gy") % 2 == 0
    beside = outer_swap(pair.reshape(180, nz), "gy").reshape(9, 2, 10, nz)
    own = jnp.where(even, pair[0::2], pair[1::2]).reshape(90, nz)
    moves = [(j + 2, j) if j % 2 == 0 else (j, j + 2) for j in range(ny - 2)]
    beyond = lax.ppermute(own, "gy", moves).reshape(9, 1, 10, nz)
    pair = pair.reshape(9, 2, 10, nz)
    return jnp.where(
        even,
        jnp.concatenate([beside, pair, beyond], axis=1),
        jnp.concatenate([beyond, pair, beside], axis=1),
    )


def per_device(density, fixed, loaded, load):
    nz = density.shape[2]
    even = lax.axis_index("gx") % 2 == 0
    args = (even.astype(jnp.int32).reshape(1), density, fixed, loaded, load)
    ins = [SMEM] + [HBM] * 4
    sems = pltpu.SemaphoreType.DMA((4,))
    outer = call(
        edge_kernel,
        [(5, 8, nz)],
        *args,
        ins=ins,
        scratch=[pltpu.VMEM((8, nz), a.dtype) for a in args[1:4]]
        + [pltpu.VMEM((3, 8, nz), F32), sems],
        limit=60,
    )
    outer = outer_swap(outer, "gx")
    fine, inner = call(
        prepare_kernel,
        [(5, 4, 8, nz), (5, 8, nz)],
        *args,
        ins=ins,
        scratch=[pltpu.VMEM(a.shape, a.dtype) for a in args[1:]] + [sems],
    )
    inner = inner_swap(inner, "gx")
    before, after = jnp.where(even, outer, inner), jnp.where(even, inner, outer)

    def edge(row):
        planes = [before[:, None, row], fine[:, :, row], after[:, None, row]]
        return jnp.concatenate(planes, axis=1).reshape(30, nz)

    rims = [r.reshape(5, 6, nz) for r in both_sides(edge(0), edge(7), "gy")]
    fine_args = (fine, before, after, *rims)
    mid = call(fine_residual_kernel, [(40, nz // 2)], *fine_args)

    sides = both_sides(mid, mid, "gx")
    shape = (5, 2, 4, nz // 2)
    mid = jnp.concatenate([a.reshape(shape) for a in (sides[0], mid, sides[1])], axis=1)
    rows_before, rows_after = both_sides(
        mid[:, :, :2].reshape(60, nz // 2), mid[:, :, 2:].reshape(60, nz // 2), "gy"
    )
    shape = (5, 6, 2, nz // 2)
    mid = jnp.concatenate(
        [rows_before.reshape(shape), mid, rows_after.reshape(shape)], axis=2
    )
    low = call(mid_residual_kernel, [(16, 10, nz // 4)], mid)
    low = gather_low(low).reshape(9, 5, 5, 2, nz // 4)
    low = low.transpose(2, 0, 1, 3, 4).reshape(5, 9, 10, nz // 4)
    low = jnp.concatenate(
        [low[:, :, 1:], jnp.zeros((5, 9, 6, nz // 4), F32), low[:, :, :1]], axis=2
    )
    return call(
        finish_kernel,
        [(3, 4, 8, nz)],
        low,
        mid,
        *fine_args,
        outs=[HBM],
        scratch=[pltpu.VMEM((3, 4, 8, nz), F32), sems],
    )


def solution(mesh):
    return jax.shard_map(
        per_device,
        mesh=mesh,
        in_specs=(
            P("gx", "gy", None),
            P("gx", "gy", None),
            P("gx", "gy", None),
            P(None, "gx", "gy", None),
        ),
        out_specs=P(None, "gx", "gy", None),
        check_vma=False,
    )
```

```python
import jax
import jax.numpy as jnp
from jax import lax
from jax.experimental import pallas as pl
from jax.experimental.pallas import tpu as pltpu
from jax.sharding import PartitionSpec as P

F32 = jnp.float32
EXTRA = 8
HBM = pl.BlockSpec(memory_space=pltpu.HBM)
SMEM = pl.BlockSpec(memory_space=pltpu.SMEM)
VMEM = pl.BlockSpec(memory_space=pltpu.VMEM)


def iota(shape, dim):
    return lax.broadcasted_iota(jnp.int32, shape, dim)


def pick_rows(a, index):
    return jnp.take_along_axis(a, index, axis=0)


def lanes(a, k):
    return a[:, 128 * k : 128 * (k + 1)]


def spread_lanes(a):
    half = iota((8, 128), 1) // 2
    tiles = []
    for k in range(a.shape[1] // 128):
        for index in (half, half + 64):
            tiles.append(jnp.take_along_axis(lanes(a, k), index, axis=1))
    return jnp.concatenate(tiles, axis=1)


def pool_lanes(a):
    a = a + pltpu.roll(a, a.shape[1] - 1, 1)
    lane = iota((8, 128), 1)
    index = lane % 64 * 2
    tiles = []
    for k in range(0, a.shape[1] // 128, 2):
        low = jnp.take_along_axis(lanes(a, k), index, axis=1)
        high = jnp.take_along_axis(lanes(a, k + 1), index, axis=1)
        tiles.append(jnp.where(lane < 64, low, high))
    return jnp.concatenate(tiles, axis=1)


def z_parts(tiles):
    t, d = [], []
    for a in tiles:
        n = a.shape[1]
        lane = iota(a.shape, 1)
        after = jnp.where(lane == n - 1, 0.0, pltpu.roll(a, n - 1, 1))
        before = jnp.where(lane == 0, 0.0, pltpu.roll(a, 1, 1))
        t.append((after + before) + 2.0 * a)
        d.append(after - before)
    return tuple(t), tuple(d)


def y_pair(tiles):
    a = tiles[0]
    n = a.shape[0]
    if len(tiles) == 1:
        return pltpu.roll(a, n - 1, 0), pltpu.roll(a, 1, 0)
    row = iota(a.shape, 0)
    after = pltpu.roll(jnp.where(row == 0, tiles[1], a), n - 1, 0)
    before = pltpu.roll(jnp.where(row == n - 1, tiles[1], a), 1, 0)
    return after, before


def y_t(tiles):
    after, before = y_pair(tiles)
    return (after + before) + 2.0 * tiles[0]


def y_d(tiles):
    after, before = y_pair(tiles)
    return after - before


def y_both(tiles):
    after, before = y_pair(tiles)
    return (after + before) + 2.0 * tiles[0], after - before


def plane_terms(v):
    (tx, dx), (ty, dy), (tz, dz) = [z_parts(c) for c in v]
    xt, xd = y_both(tx)
    xc = y_t(dx)
    yt, yd = y_both(ty)
    yc = y_d(dy)
    zt = y_t(tz)
    zb, zc = y_both(dz)
    return (
        (xt, yt + 0.25 * zc, zt + 0.25 * yc),
        (0.25 * (yd + zb), 0.25 * xd, 0.25 * xc),
    )


def scalar_terms(s):
    t, _ = z_parts(s)
    return y_t(t)


def times(a, b):
    return tuple(p * q for p, q in zip(a, b))


def stiff_sums(s, planes):
    terms = {p: scalar_terms(s[p]) for p in range(planes[0] - 1, planes[-1] + 2)}
    return {p: 2.0 * terms[p] + (terms[p + 1] + terms[p - 1]) for p in planes}


def stencil(v, s, sums, planes, use=None):
    own, scaled = {}, {}
    result = {}
    for p in range(planes[0] - 1, planes[-1] + 2):
        for store, field in ((own, v[p]), (scaled, [times(c, s[p]) for c in v[p]])):
            even, odd = plane_terms(field)
            store[p] = (
                [2.0 * e for e in even],
                [e + o for e, o in zip(even, odd)],
                [e - o for e, o in zip(even, odd)],
            )
        q = p - 1
        if q in planes:
            here = []
            for c in range(3):
                plain = own[q][0][c] + (own[q + 1][1][c] + own[q - 1][2][c])
                heavy = scaled[q][0][c] + (scaled[q + 1][1][c] + scaled[q - 1][2][c])
                u, k = v[q][c][0], s[q][0]
                here.append(8.1 * (k * u) + 0.125 * (u * sums[q] - (k * plain + heavy)))
            result[q] = here
            if use is not None:
                use(q, here)
    return result


def gain(stiff, free):
    return free * 0.8 / (7.1 * stiff + 7.5)


def run_copies(pairs, sems):
    copies = [
        pltpu.make_async_copy(source, target, sems.at[k])
        for k, (source, target) in enumerate(pairs)
    ]
    for copy in copies:
        copy.start()
    for copy in copies:
        copy.wait()


def start_values(density, fixed, loaded, load):
    level = (density.astype(F32) + 1.0) * (1.0 / 256.0)
    stiff = 0.05 + level * level * level
    free = (1 - fixed).astype(F32)
    factor = gain(stiff, free) * loaded.astype(F32)
    return [factor * c for c in load] + [stiff, free]


def edge_kernel(even, density, fixed, loaded, load, outer, *scratch):
    plane = jnp.where(even[0] == 1, 0, 3)
    sources = [a.at[plane] for a in (density, fixed, loaded)] + [load.at[:, plane]]
    run_copies(zip(sources, scratch[:4]), scratch[4])
    d, x, m, f = scratch[:4]
    values = start_values(d[...], x[...], m[...], [f[c] for c in range(3)])
    for k in range(5):
        outer[k] = values[k]


def prepare_kernel(even, density, fixed, loaded, load, fine, inner, *scratch):
    run_copies(zip((density, fixed, loaded, load), scratch[:4]), scratch[4])
    d, x, m, f = scratch[:4]
    is_even = even[0] == 1
    kept = {}
    for p in range(4):
        values = start_values(d[p], x[p], m[p], [f[c, p] for c in range(3)])
        for k in range(5):
            fine[k, p] = values[k]
        kept[p] = values
    for k in range(5):
        inner[k] = jnp.where(is_even, kept[3][k], kept[0][k])


def fine_tiles(fine, before, after, row_before, row_after):
    row = iota((8, fine.shape[3]), 0)
    result = []
    for p in range(6):
        here = []
        for f in range(5):
            main = before[f] if p == 0 else after[f] if p == 5 else fine[f, p - 1]
            rim = jnp.where(
                row == 0, row_after[f, pl.ds(p, 1), :], row_before[f, pl.ds(p, 1), :]
            )
            here.append((main, rim))
        result.append(here)
    return result


def fine_residual_kernel(fine, before, after, row_before, row_after, mid):
    tiles = fine_tiles(fine, before, after, row_before, row_after)
    v = [t[:3] for t in tiles]
    s = [t[3] for t in tiles]
    planes = range(1, 5)
    image = stencil(v, s, stiff_sums(s, planes), planes)
    rows = [[], [], [], [], []]
    for p in planes:
        stiff, free = s[p][0], tiles[p][4][0]
        back = 1.25 * (7.1 * stiff + 7.5)
        for c in range(3):
            rows[c].append(free * (back * v[p][c][0] - image[p][c]))
        rows[3].append(stiff)
        rows[4].append(free)
    row = iota((8, rows[0][0].shape[1]), 0)
    index = row % 4 * 2
    for f in range(5):
        halves = []
        for x in (0, 2):
            both = rows[f][x] + rows[f][x + 1]
            halves.append(pick_rows(both + pltpu.roll(both, 7, 0), index))
        total = pool_lanes(jnp.where(row < 4, halves[0], halves[1]))
        if f == 3:
            total = total * 0.125
        if f == 4:
            total = (total > 0.5).astype(F32)
        mid[8 * f : 8 * f + 8] = total


def mid_fields(mids):
    v, s, free, gains = [], [], [], []
    for p in range(6):
        mid = mids[p // 2].at[:, p % 2]
        stiff, open_ = mid[3], mid[4]
        g = gain(stiff, open_)
        v.append([(0.5 * g * mid[c],) for c in range(3)])
        s.append((stiff,))
        free.append(open_)
        gains.append(g)
    return v, s, free, gains


def mid_residual_kernel(before, mid, after, low):
    v, s, free, _ = mid_fields((before, mid, after))
    planes = range(2, 4)
    image = stencil(v, s, stiff_sums(s, planes), planes)
    pairs = []
    for c in range(3):
        pairs.append(
            sum(free[p] * (mid[c, p - 2] - 2.0 * image[p][c]) for p in planes)
        )
    pairs.append(s[2][0] + s[3][0])
    pairs.append(free[2] + free[3])
    sums = [pool_lanes(a + pltpu.roll(a, 7, 0)) for a in pairs]
    sums[3] = sums[3] * 0.125
    sums[4] = (sums[4] > 0.5).astype(F32)
    row = iota(sums[0].shape, 0)
    index = 2 + row % 2 * 2
    packed = pick_rows(sums[0], index)
    for f in range(1, 4):
        packed = jnp.where(row // 2 == f, pick_rows(sums[f], index), packed)
    last = pick_rows(sums[4], index)[0:2]
    for k in range(low.shape[0]):
        low[k, 0:8] = packed
        low[k, 8:10] = last


def finish_kernel(
    low,
    mid_before,
    mid,
    mid_after,
    fine,
    before,
    after,
    row_before,
    row_after,
    out,
    held,
    sems,
):
    parts = [slice(0, 8), slice(8, 16)]
    s = [tuple(low[3, p, k] for k in parts) for p in range(9)]
    gains = [tuple(gain(low[3, p, k], low[4, p, k]) for k in parts) for p in range(9)]
    first = [
        [tuple(0.25 * gains[p][k] * low[c, p, parts[k]] for k in range(2)) for c in range(3)]
        for p in range(9)
    ]
    v = dict(enumerate(first))
    sums = stiff_sums(s, range(1, 8))
    for reach in (1, 2, 3):
        planes = range(reach, 9 - reach)
        image = stencil(v, s, sums, planes)
        v = {
            p: [
                (v[p][c][0] + first[p][c][0] - gains[p][0] * image[p][c],)
                for c in range(3)
            ]
            for p in planes
        }
    row = iota((8, low.shape[3]), 0)
    raised = [
        [spread_lanes(pick_rows(v[p][c][0], 2 + row // 2)) for p in (3, 4, 5)]
        for c in range(3)
    ]
    first, s, free, gains = mid_fields((mid_before, mid, mid_after))
    v = []
    for p in range(6):
        here = []
        for c in range(3):
            here.append((first[p][c][0] + free[p] * raised[c][p // 2],))
        v.append(here)
    planes = range(1, 5)
    image = stencil(v, s, stiff_sums(s, planes), planes)
    row = iota((8, mid.shape[3]), 0)
    picks = (2 + row // 2, jnp.where(row == 0, 6, 1))
    raised = []
    for c in range(3):
        raised.append([])
        for p in planes:
            a = v[p][c][0] + first[p][c][0] - gains[p] * image[p][c]
            raised[c].append([spread_lanes(pick_rows(a, index)) for index in picks])
    tiles = fine_tiles(fine, before, after, row_before, row_after)
    s = [t[3] for t in tiles]
    v = []
    for p in range(6):
        here = []
        for c in range(3):
            up = raised[c][(p + 1) // 2]
            here.append(
                tuple(tiles[p][c][k] + tiles[p][4][k] * up[k] for k in range(2))
            )
        v.append(here)
    sums = stiff_sums(s, planes)
    copies = []

    def finish(p, image):
        g = gain(s[p][0], tiles[p][4][0])
        for c in range(3):
            held[c, p - 1] = v[p][c][0] + tiles[p][c][0] - g * image[c]
        copies.append(
            pltpu.make_async_copy(held.at[:, p - 1], out.at[:, p - 1], sems.at[p - 1])
        )
        copies[-1].start()

    stencil(v, s, sums, planes, finish)
    for copy in copies:
        copy.wait()


def call(kernel, shapes, *args, ins=None, outs=None, scratch=(), limit=48):
    results = [jax.ShapeDtypeStruct(shape, F32) for shape in shapes]
    outs = outs or [VMEM] * len(results)
    return pl.pallas_call(
        kernel,
        out_shape=results if len(results) > 1 else results[0],
        in_specs=ins or [VMEM] * len(args),
        out_specs=outs if len(results) > 1 else outs[0],
        scratch_shapes=list(scratch),
        compiler_params=pltpu.CompilerParams(vmem_limit_bytes=limit << 20),
    )(*args)


def inner_swap(value, axis):
    return lax.ppermute(value, axis, [(i, i ^ 1) for i in range(lax.axis_size(axis))])


def outer_swap(value, axis):
    n = lax.axis_size(axis)
    return lax.ppermute(
        value, axis, [(i, ((i + 1) ^ 1) - 1) for i in range(1, n - 1)]
    )


def shifts(low, high, axis):
    n = lax.axis_size(axis)
    rows = low.shape[0]
    low = jnp.concatenate([low, low[:EXTRA]])
    after = lax.ppermute(low, axis, [(i + 1, i) for i in range(n - 1)])[:rows]
    before = lax.ppermute(high, axis, [(i, i + 1) for i in range(n - 1)])
    return before, after


def swaps(value, axis):
    even = lax.axis_index(axis) % 2 == 0
    outer = outer_swap(jnp.concatenate([value, value[:EXTRA]]), axis)[: value.shape[0]]
    inner = inner_swap(value, axis)
    return jnp.where(even, outer, inner), jnp.where(even, inner, outer)


def gather_low(low):
    nx, ny = lax.axis_size("gx"), lax.axis_size("gy")
    nz = low.shape[2]
    groups = [
        [(8 * g + i) * ny + 2 * h + j for i in range(8) for j in range(2)]
        for g in range(nx // 8)
        for h in range(ny // 2)
    ]
    row = lax.all_to_all(low, ("gx", "gy"), 0, 0, axis_index_groups=groups)
    place = lax.axis_index("gx") % 8
    first = place < 4
    moves = [(j, j + 8) for j in range(nx - 8) if j % 8 < 4]
    moves += [(j, j - 8) for j in range(8, nx) if j % 8 >= 4]
    other = lax.ppermute(jnp.where(first, row[8:], row[:8]), "gx", moves)
    planes = jnp.where(
        first, jnp.concatenate([other, row]), jnp.concatenate([row, other])
    )
    pair = lax.dynamic_slice_in_dim(planes, place % 4 * 2, 18, 0)
    even = lax.axis_index("gy") % 2 == 0
    beside = outer_swap(pair.reshape(180, nz), "gy").reshape(9, 2, 10, nz)
    own = jnp.where(even, pair[0::2], pair[1::2]).reshape(90, nz)
    moves = [(j + 2, j) if j % 2 == 0 else (j, j + 2) for j in range(ny - 2)]
    beyond = lax.ppermute(own, "gy", moves).reshape(9, 1, 10, nz)
    pair = pair.reshape(9, 2, 10, nz)
    return jnp.where(
        even,
        jnp.concatenate([beside, pair, beyond], axis=1),
        jnp.concatenate([beyond, pair, beside], axis=1),
    )


def per_device(density, fixed, loaded, load):
    nz = density.shape[2]
    even = lax.axis_index("gx") % 2 == 0
    args = (even.astype(jnp.int32).reshape(1), density, fixed, loaded, load)
    ins = [SMEM] + [HBM] * 4
    sems = pltpu.SemaphoreType.DMA((4,))
    outer = call(
        edge_kernel,
        [(5, 8, nz)],
        *args,
        ins=ins,
        scratch=[pltpu.VMEM((8, nz), a.dtype) for a in args[1:4]]
        + [pltpu.VMEM((3, 8, nz), F32), sems],
        limit=60,
    )
    outer = outer_swap(outer, "gx")
    fine, inner = call(
        prepare_kernel,
        [(5, 4, 8, nz), (5, 8, nz)],
        *args,
        ins=ins,
        scratch=[pltpu.VMEM(a.shape, a.dtype) for a in args[1:]] + [sems],
    )
    inner = inner_swap(inner, "gx")
    before, after = jnp.where(even, outer, inner), jnp.where(even, inner, outer)

    def edge(row):
        planes = [before[:, None, row], fine[:, :, row], after[:, None, row]]
        return jnp.concatenate(planes, axis=1).reshape(30, nz)

    rims = [r.reshape(5, 6, nz) for r in shifts(edge(0), edge(7), "gy")]
    fine_args = (fine, before, after, *rims)
    mid = call(fine_residual_kernel, [(40, nz // 2)], *fine_args)

    mid = mid.reshape(5, 2, 4, nz // 2)
    rows = shifts(
        mid[:, :, :2].reshape(20, nz // 2), mid[:, :, 2:].reshape(20, nz // 2), "gy"
    )
    rows = [r.reshape(5, 2, 2, nz // 2) for r in rows]
    mid = jnp.concatenate([rows[0], mid, rows[1]], axis=2).reshape(80, nz // 2)
    sides = swaps(mid, "gx")
    mids = [a.reshape(5, 2, 8, nz // 2) for a in (sides[0], mid, sides[1])]
    low = call(mid_residual_kernel, [(16, 10, nz // 4)], *mids)
    low = gather_low(low).reshape(9, 5, 5, 2, nz // 4)
    low = low.transpose(2, 0, 1, 3, 4).reshape(5, 9, 10, nz // 4)
    low = jnp.concatenate(
        [low[:, :, 1:], jnp.zeros((5, 9, 6, nz // 4), F32), low[:, :, :1]], axis=2
    )
    return call(
        finish_kernel,
        [(3, 4, 8, nz)],
        low,
        *mids,
        *fine_args,
        outs=[HBM],
        scratch=[pltpu.VMEM((3, 4, 8, nz), F32), sems],
    )


def solution(mesh):
    return jax.shard_map(
        per_device,
        mesh=mesh,
        in_specs=(
            P("gx", "gy", None),
            P("gx", "gy", None),
            P("gx", "gy", None),
            P(None, "gx", "gy", None),
        ),
        out_specs=P(None, "gx", "gy", None),
        check_vma=False,
    )
```

```python
import jax
import jax.numpy as jnp
from jax import lax
from jax.experimental import pallas as pl
from jax.experimental.pallas import tpu as pltpu
from jax.sharding import PartitionSpec as P

F32 = jnp.float32
EXTRA = 8
HBM = pl.BlockSpec(memory_space=pltpu.HBM)
SMEM = pl.BlockSpec(memory_space=pltpu.SMEM)
VMEM = pl.BlockSpec(memory_space=pltpu.VMEM)


def iota(shape, dim):
    return lax.broadcasted_iota(jnp.int32, shape, dim)


def pick_rows(a, index):
    return jnp.take_along_axis(a, index, axis=0)


def lanes(a, k):
    return a[:, 128 * k : 128 * (k + 1)]


def spread_lanes(a):
    half = iota((8, 128), 1) // 2
    tiles = []
    for k in range(a.shape[1] // 128):
        for index in (half, half + 64):
            tiles.append(jnp.take_along_axis(lanes(a, k), index, axis=1))
    return jnp.concatenate(tiles, axis=1)


def pool_lanes(a):
    a = a + pltpu.roll(a, a.shape[1] - 1, 1)
    lane = iota((8, 128), 1)
    index = lane % 64 * 2
    tiles = []
    for k in range(0, a.shape[1] // 128, 2):
        low = jnp.take_along_axis(lanes(a, k), index, axis=1)
        high = jnp.take_along_axis(lanes(a, k + 1), index, axis=1)
        tiles.append(jnp.where(lane < 64, low, high))
    return jnp.concatenate(tiles, axis=1)


def z_parts(tiles):
    t, d = [], []
    for a in tiles:
        n = a.shape[1]
        lane = iota(a.shape, 1)
        after = jnp.where(lane == n - 1, 0.0, pltpu.roll(a, n - 1, 1))
        before = jnp.where(lane == 0, 0.0, pltpu.roll(a, 1, 1))
        t.append((after + before) + 2.0 * a)
        d.append(after - before)
    return tuple(t), tuple(d)


def y_pair(tiles):
    a = tiles[0]
    n = a.shape[0]
    if len(tiles) == 1:
        return pltpu.roll(a, n - 1, 0), pltpu.roll(a, 1, 0)
    row = iota(a.shape, 0)
    rim = tiles[1] if n == 8 else jnp.concatenate([tiles[1]] * 2, axis=0)
    after = pltpu.roll(jnp.where(row == 0, rim, a), n - 1, 0)
    before = pltpu.roll(jnp.where(row == n - 1, rim, a), 1, 0)
    return after, before


def y_t(tiles):
    after, before = y_pair(tiles)
    return (after + before) + 2.0 * tiles[0]


def y_d(tiles):
    after, before = y_pair(tiles)
    return after - before


def y_both(tiles):
    after, before = y_pair(tiles)
    return (after + before) + 2.0 * tiles[0], after - before


def plane_terms(v):
    (tx, dx), (ty, dy), (tz, dz) = [z_parts(c) for c in v]
    xt, xd = y_both(tx)
    xc = y_t(dx)
    yt, yd = y_both(ty)
    yc = y_d(dy)
    zt = y_t(tz)
    zb, zc = y_both(dz)
    return (
        (xt, yt + 0.25 * zc, zt + 0.25 * yc),
        (0.25 * (yd + zb), 0.25 * xd, 0.25 * xc),
    )


def scalar_terms(s):
    t, _ = z_parts(s)
    return y_t(t)


def times(a, b):
    return tuple(p * q for p, q in zip(a, b))


def stiff_sums(s, planes):
    terms = {p: scalar_terms(s[p]) for p in range(planes[0] - 1, planes[-1] + 2)}
    return {p: 2.0 * terms[p] + (terms[p + 1] + terms[p - 1]) for p in planes}


def stencil(v, s, sums, planes, use=None):
    own, scaled = {}, {}
    result = {}
    for p in range(planes[0] - 1, planes[-1] + 2):
        for store, field in ((own, v[p]), (scaled, [times(c, s[p]) for c in v[p]])):
            even, odd = plane_terms(field)
            store[p] = (
                [2.0 * e for e in even],
                [e + o for e, o in zip(even, odd)],
                [e - o for e, o in zip(even, odd)],
            )
        q = p - 1
        if q in planes:
            here = []
            for c in range(3):
                plain = own[q][0][c] + (own[q + 1][1][c] + own[q - 1][2][c])
                heavy = scaled[q][0][c] + (scaled[q + 1][1][c] + scaled[q - 1][2][c])
                u, k = v[q][c][0], s[q][0]
                here.append(8.1 * (k * u) + 0.125 * (u * sums[q] - (k * plain + heavy)))
            result[q] = here
            if use is not None:
                use(q, here)
    return result


def gain(stiff, free):
    return free * 0.8 / (7.1 * stiff + 7.5)


def run_copies(pairs, sems):
    copies = [
        pltpu.make_async_copy(source, target, sems.at[k])
        for k, (source, target) in enumerate(pairs)
    ]
    for copy in copies:
        copy.start()
    for copy in copies:
        copy.wait()


def start_values(density, fixed, loaded, load):
    level = (density.astype(F32) + 1.0) * (1.0 / 256.0)
    stiff = 0.05 + level * level * level
    free = (1 - fixed).astype(F32)
    factor = gain(stiff, free) * loaded.astype(F32)
    return [factor * c for c in load] + [stiff, free]


def rows_kernel(density, fixed, loaded, load, low, high, *scratch):
    run_copies(zip((density, fixed, loaded, load), scratch[:4]), scratch[4])
    d, x, m, f = scratch[:4]
    low[0:8] = jnp.zeros((8, low.shape[1]), F32)
    high[96:104] = jnp.zeros((8, low.shape[1]), F32)
    for p in range(4):
        values = start_values(d[p], x[p], m[p], [f[c, p] for c in range(3)])
        for k in range(5):
            at = 5 * (4 * k + p)
            low[8 + at : 13 + at] = values[k][0:5]
            high[at : at + 5] = values[k][3:8]


def fine_kernel(density, fixed, loaded, load, fine, *scratch):
    run_copies(zip((density, fixed, loaded, load), scratch[:4]), scratch[4])
    d, x, m, f = scratch[:4]
    for p in range(4):
        values = start_values(d[p], x[p], m[p], [f[c, p] for c in range(3)])
        for k in range(5):
            fine[k, p] = values[k]


def rim_tile(after, before):
    row = iota((8, after.shape[1]), 0)
    return jnp.where(row == 0, after, before)


def own_rows(fine, low, high, k, p):
    at = 5 * (4 * k + p)
    row = iota((8, fine.shape[3]), 0)
    turned = pltpu.roll(fine[k, p], 4, 0)
    first = jnp.where(row < 4, high[at + 1 : at + 9], turned)
    last = jnp.where(row < 4, turned, low[at + 4 : at + 12])
    rim = rim_tile(low[at + 12 : at + 13], high[at : at + 1])
    return jnp.concatenate([first, last], axis=0), rim


def side_rows(side, k):
    at = 80 + 2 * k
    rim = rim_tile(side[at + 1 : at + 2], side[at : at + 1])
    return side[16 * k : 16 * k + 16], rim


def sides_kernel(even, fine, low, high, outer, inner):
    is_even = even[0] == 1
    for k in range(5):
        first, last = [own_rows(fine, low, high, k, p)[0] for p in (0, 3)]
        outer[16 * k : 16 * k + 16] = jnp.where(is_even, first, last)
        inner[16 * k : 16 * k + 16] = jnp.where(is_even, last, first)
        ends = []
        for p in (0, 3):
            at = 5 * (4 * k + p)
            ends.append((high[at : at + 1], low[at + 12 : at + 13]))
        for j in range(2):
            first, last = ends[0][j], ends[1][j]
            at = 80 + 2 * k + j
            outer[at : at + 1] = jnp.where(is_even, first, last)
            inner[at : at + 1] = jnp.where(is_even, last, first)
    outer[90:104] = jnp.zeros((14, low.shape[1]), F32)
    inner[90:96] = jnp.zeros((6, low.shape[1]), F32)


def fine_tiles(fine, low, high, before, after):
    result = []
    for p in range(6):
        here = []
        for k in range(5):
            if p in (0, 5):
                side, at = before if p == 0 else after, 16 * k
                main = side[at + 4 : at + 12]
                rim = rim_tile(side[at + 12 : at + 13], side[at + 3 : at + 4])
            else:
                at = 5 * (4 * k + p - 1)
                main = fine[k, p - 1]
                rim = rim_tile(low[at + 8 : at + 9], high[at + 4 : at + 5])
            here.append((main, rim))
        result.append(here)
    return result


def fine_residual_kernel(fine, low, high, before, after, mid):
    tiles = []
    for p in range(6):
        if p in (0, 5):
            side = before if p == 0 else after
            tiles.append([side_rows(side, k) for k in range(5)])
        else:
            tiles.append([own_rows(fine, low, high, k, p - 1) for k in range(5)])
    v = [t[:3] for t in tiles]
    s = [t[3] for t in tiles]
    planes = range(1, 5)
    image = stencil(v, s, stiff_sums(s, planes), planes)
    rows = [[], [], [], [], []]
    for p in planes:
        stiff, free = s[p][0], tiles[p][4][0]
        back = 1.25 * (7.1 * stiff + 7.5)
        for c in range(3):
            rows[c].append(free * (back * v[p][c][0] - image[p][c]))
        rows[3].append(stiff)
        rows[4].append(free)
    row = iota((8, fine.shape[3]), 0)
    index = row % 4 * 2
    for f in range(5):
        for x in (0, 2):
            both = rows[f][x] + rows[f][x + 1]
            both = both + pltpu.roll(both, 15, 0)
            halves = [pick_rows(both[at : at + 8], index) for at in (0, 8)]
            total = pool_lanes(jnp.where(row < 4, halves[0], halves[1]))
            if f == 3:
                total = total * 0.125
            if f == 4:
                total = (total > 0.5).astype(F32)
            at = 16 * f + 4 * x
            mid[at : at + 8] = total


def mid_fields(mids):
    v, s, free, gains = [], [], [], []
    for p in range(6):
        mid = mids[p // 2].at[:, p % 2]
        stiff, open_ = mid[3], mid[4]
        g = gain(stiff, open_)
        v.append([(0.5 * g * mid[c],) for c in range(3)])
        s.append((stiff,))
        free.append(open_)
        gains.append(g)
    return v, s, free, gains


def mid_residual_kernel(before, mid, after, low):
    v, s, free, _ = mid_fields((before, mid, after))
    planes = range(2, 4)
    image = stencil(v, s, stiff_sums(s, planes), planes)
    pairs = []
    for c in range(3):
        pairs.append(
            sum(free[p] * (mid[c, p - 2] - 2.0 * image[p][c]) for p in planes)
        )
    pairs.append(s[2][0] + s[3][0])
    pairs.append(free[2] + free[3])
    sums = [pool_lanes(a + pltpu.roll(a, 7, 0)) for a in pairs]
    sums[3] = sums[3] * 0.125
    sums[4] = (sums[4] > 0.5).astype(F32)
    row = iota(sums[0].shape, 0)
    index = 2 + row % 2 * 2
    packed = pick_rows(sums[0], index)
    for f in range(1, 4):
        packed = jnp.where(row // 2 == f, pick_rows(sums[f], index), packed)
    last = pick_rows(sums[4], index)[0:2]
    for k in range(low.shape[0]):
        low[k, 0:8] = packed
        low[k, 8:10] = last


def finish_kernel(
    low,
    mid_before,
    mid,
    mid_after,
    fine,
    row_after,
    row_before,
    before,
    after,
    out,
    held,
    sems,
):
    parts = [slice(0, 8), slice(8, 16)]
    s = [tuple(low[3, p, k] for k in parts) for p in range(9)]
    gains = [tuple(gain(low[3, p, k], low[4, p, k]) for k in parts) for p in range(9)]
    first = [
        [tuple(0.25 * gains[p][k] * low[c, p, parts[k]] for k in range(2)) for c in range(3)]
        for p in range(9)
    ]
    v = dict(enumerate(first))
    sums = stiff_sums(s, range(1, 8))
    for reach in (1, 2, 3):
        planes = range(reach, 9 - reach)
        image = stencil(v, s, sums, planes)
        v = {
            p: [
                (v[p][c][0] + first[p][c][0] - gains[p][0] * image[p][c],)
                for c in range(3)
            ]
            for p in planes
        }
    row = iota((8, low.shape[3]), 0)
    raised = [
        [spread_lanes(pick_rows(v[p][c][0], 2 + row // 2)) for p in (3, 4, 5)]
        for c in range(3)
    ]
    first, s, free, gains = mid_fields((mid_before, mid, mid_after))
    v = []
    for p in range(6):
        here = []
        for c in range(3):
            here.append((first[p][c][0] + free[p] * raised[c][p // 2],))
        v.append(here)
    planes = range(1, 5)
    image = stencil(v, s, stiff_sums(s, planes), planes)
    row = iota((8, mid.shape[3]), 0)
    picks = (2 + row // 2, jnp.where(row == 0, 6, 1))
    raised = []
    for c in range(3):
        raised.append([])
        for p in planes:
            a = v[p][c][0] + first[p][c][0] - gains[p] * image[p][c]
            raised[c].append([spread_lanes(pick_rows(a, index)) for index in picks])
    tiles = fine_tiles(fine, row_after, row_before, before, after)
    s = [t[3] for t in tiles]
    v = []
    for p in range(6):
        here = []
        for c in range(3):
            up = raised[c][(p + 1) // 2]
            here.append(
                tuple(tiles[p][c][k] + tiles[p][4][k] * up[k] for k in range(2))
            )
        v.append(here)
    sums = stiff_sums(s, planes)
    copies = []

    def finish(p, image):
        g = gain(s[p][0], tiles[p][4][0])
        for c in range(3):
            held[c, p - 1] = v[p][c][0] + tiles[p][c][0] - g * image[c]
        copies.append(
            pltpu.make_async_copy(held.at[:, p - 1], out.at[:, p - 1], sems.at[p - 1])
        )
        copies[-1].start()

    stencil(v, s, sums, planes, finish)
    for copy in copies:
        copy.wait()


def call(kernel, shapes, *args, ins=None, outs=None, scratch=(), limit=48):
    results = [jax.ShapeDtypeStruct(shape, F32) for shape in shapes]
    outs = outs or [VMEM] * len(results)
    return pl.pallas_call(
        kernel,
        out_shape=results if len(results) > 1 else results[0],
        in_specs=ins or [VMEM] * len(args),
        out_specs=outs if len(results) > 1 else outs[0],
        scratch_shapes=list(scratch),
        compiler_params=pltpu.CompilerParams(vmem_limit_bytes=limit << 20),
    )(*args)


def inner_swap(value, axis):
    return lax.ppermute(value, axis, [(i, i ^ 1) for i in range(lax.axis_size(axis))])


def outer_swap(value, axis):
    n = lax.axis_size(axis)
    return lax.ppermute(
        value, axis, [(i, ((i + 1) ^ 1) - 1) for i in range(1, n - 1)]
    )


def swaps(value, axis):
    even = lax.axis_index(axis) % 2 == 0
    outer = outer_swap(jnp.concatenate([value, value[:EXTRA]]), axis)[: value.shape[0]]
    inner = inner_swap(value, axis)
    return jnp.where(even, outer, inner), jnp.where(even, inner, outer)


def gather_low(low):
    nx, ny = lax.axis_size("gx"), lax.axis_size("gy")
    nz = low.shape[2]
    groups = [
        [(8 * g + i) * ny + 2 * h + j for i in range(8) for j in range(2)]
        for g in range(nx // 8)
        for h in range(ny // 2)
    ]
    row = lax.all_to_all(low, ("gx", "gy"), 0, 0, axis_index_groups=groups)
    place = lax.axis_index("gx") % 8
    first = place < 4
    moves = [(j, j + 8) for j in range(nx - 8) if j % 8 < 4]
    moves += [(j, j - 8) for j in range(8, nx) if j % 8 >= 4]
    other = lax.ppermute(jnp.where(first, row[8:], row[:8]), "gx", moves)
    planes = jnp.where(
        first, jnp.concatenate([other, row]), jnp.concatenate([row, other])
    )
    pair = lax.dynamic_slice_in_dim(planes, place % 4 * 2, 18, 0)
    even = lax.axis_index("gy") % 2 == 0
    beside = outer_swap(pair.reshape(180, nz), "gy").reshape(9, 2, 10, nz)
    own = jnp.where(even, pair[0::2], pair[1::2]).reshape(90, nz)
    moves = [(j + 2, j) if j % 2 == 0 else (j, j + 2) for j in range(ny - 2)]
    beyond = lax.ppermute(own, "gy", moves).reshape(9, 1, 10, nz)
    pair = pair.reshape(9, 2, 10, nz)
    return jnp.where(
        even,
        jnp.concatenate([beside, pair, beyond], axis=1),
        jnp.concatenate([beyond, pair, beside], axis=1),
    )


def per_device(density, fixed, loaded, load):
    nz = density.shape[2]
    args = (density, fixed, loaded, load)
    sems = pltpu.SemaphoreType.DMA((4,))
    inputs = dict(
        ins=[HBM] * 4, scratch=[pltpu.VMEM(a.shape, a.dtype) for a in args] + [sems]
    )
    low_rows, high_rows = call(
        rows_kernel, [(108, nz), (104, nz)], *args, limit=60, **inputs
    )
    n = lax.axis_size("gy")
    row_after = lax.ppermute(low_rows, "gy", [(i + 1, i) for i in range(n - 1)])
    row_before = lax.ppermute(high_rows, "gy", [(i, i + 1) for i in range(n - 1)])
    fine = call(fine_kernel, [(5, 4, 8, nz)], *args, **inputs)

    even = lax.axis_index("gx") % 2 == 0
    outer, inner = call(
        sides_kernel,
        [(104, nz), (96, nz)],
        even.astype(jnp.int32).reshape(1),
        fine,
        row_after,
        row_before,
        ins=[SMEM] + [VMEM] * 3,
    )
    outer, inner = outer_swap(outer, "gx")[:96], inner_swap(inner, "gx")
    before, after = jnp.where(even, outer, inner), jnp.where(even, inner, outer)
    fine_args = (fine, row_after, row_before, before, after)
    mid = call(fine_residual_kernel, [(80, nz // 2)], *fine_args)

    sides = swaps(mid, "gx")
    mids = [a.reshape(5, 2, 8, nz // 2) for a in (sides[0], mid, sides[1])]
    low = call(mid_residual_kernel, [(16, 10, nz // 4)], *mids)
    low = gather_low(low).reshape(9, 5, 5, 2, nz // 4)
    low = low.transpose(2, 0, 1, 3, 4).reshape(5, 9, 10, nz // 4)
    low = jnp.concatenate(
        [low[:, :, 1:], jnp.zeros((5, 9, 6, nz // 4), F32), low[:, :, :1]], axis=2
    )
    return call(
        finish_kernel,
        [(3, 4, 8, nz)],
        low,
        *mids,
        *fine_args,
        outs=[HBM],
        scratch=[pltpu.VMEM((3, 4, 8, nz), F32), sems],
    )


def solution(mesh):
    return jax.shard_map(
        per_device,
        mesh=mesh,
        in_specs=(
            P("gx", "gy", None),
            P("gx", "gy", None),
            P("gx", "gy", None),
            P(None, "gx", "gy", None),
        ),
        out_specs=P(None, "gx", "gy", None),
        check_vma=False,
    )
```

```python
import jax
import jax.numpy as jnp
from jax import lax
from jax.experimental import pallas as pl
from jax.experimental.pallas import tpu as pltpu
from jax.sharding import PartitionSpec as P

F32 = jnp.float32
EXTRA = 8
HBM = pl.BlockSpec(memory_space=pltpu.HBM)
SMEM = pl.BlockSpec(memory_space=pltpu.SMEM)
VMEM = pl.BlockSpec(memory_space=pltpu.VMEM)


def iota(shape, dim):
    return lax.broadcasted_iota(jnp.int32, shape, dim)


def pick_rows(a, index):
    return jnp.take_along_axis(a, index, axis=0)


def lanes(a, k):
    return a[:, 128 * k : 128 * (k + 1)]


def spread_lanes(a):
    half = iota((8, 128), 1) // 2
    tiles = []
    for k in range(a.shape[1] // 128):
        for index in (half, half + 64):
            tiles.append(jnp.take_along_axis(lanes(a, k), index, axis=1))
    return jnp.concatenate(tiles, axis=1)


def pool_lanes(a):
    a = a + pltpu.roll(a, a.shape[1] - 1, 1)
    lane = iota((8, 128), 1)
    index = lane % 64 * 2
    tiles = []
    for k in range(0, a.shape[1] // 128, 2):
        low = jnp.take_along_axis(lanes(a, k), index, axis=1)
        high = jnp.take_along_axis(lanes(a, k + 1), index, axis=1)
        tiles.append(jnp.where(lane < 64, low, high))
    return jnp.concatenate(tiles, axis=1)


def z_parts(tiles):
    t, d = [], []
    for a in tiles:
        n = a.shape[1]
        after, before = pltpu.roll(a, n - 1, 1), pltpu.roll(a, 1, 1)
        lane = iota((a.shape[0], 128), 1)
        last = jnp.where(lane == 127, 0.0, after[:, n - 128 :])
        first = jnp.where(lane == 0, 0.0, before[:, :128])
        if n > 128:
            last = jnp.concatenate([after[:, : n - 128], last], axis=1)
            first = jnp.concatenate([first, before[:, 128:]], axis=1)
        after, before = last, first
        t.append((after + before) + 2.0 * a)
        d.append(after - before)
    return tuple(t), tuple(d)


def y_pair(tiles):
    a = tiles[0]
    n = a.shape[0]
    if len(tiles) == 1:
        return pltpu.roll(a, n - 1, 0), pltpu.roll(a, 1, 0)
    row = iota(a.shape, 0)
    rim = tiles[1] if n == 8 else jnp.concatenate([tiles[1]] * 2, axis=0)
    after = pltpu.roll(jnp.where(row == 0, rim, a), n - 1, 0)
    before = pltpu.roll(jnp.where(row == n - 1, rim, a), 1, 0)
    return after, before


def y_t(tiles):
    after, before = y_pair(tiles)
    return (after + before) + 2.0 * tiles[0]


def y_d(tiles):
    after, before = y_pair(tiles)
    return after - before


def y_both(tiles):
    after, before = y_pair(tiles)
    return (after + before) + 2.0 * tiles[0], after - before


def plane_terms(v):
    (tx, dx), (ty, dy), (tz, dz) = [z_parts(c) for c in v]
    xt, xd = y_both(tx)
    xc = y_t(dx)
    yt, yd = y_both(ty)
    yc = y_d(dy)
    zt = y_t(tz)
    zb, zc = y_both(dz)
    return (
        (xt, yt + 0.25 * zc, zt + 0.25 * yc),
        (0.25 * (yd + zb), 0.25 * xd, 0.25 * xc),
    )


def scalar_terms(s):
    t, _ = z_parts(s)
    return y_t(t)


def times(a, b):
    return tuple(p * q for p, q in zip(a, b))


def stiff_sums(s, planes):
    terms = {p: scalar_terms(s[p]) for p in range(planes[0] - 1, planes[-1] + 2)}
    return {p: 2.0 * terms[p] + (terms[p + 1] + terms[p - 1]) for p in planes}


def stencil(v, s, sums, planes, use=None):
    own, scaled = {}, {}
    result = {}
    for p in range(planes[0] - 1, planes[-1] + 2):
        for store, field in ((own, v[p]), (scaled, [times(c, s[p]) for c in v[p]])):
            even, odd = plane_terms(field)
            store[p] = (
                [2.0 * e for e in even],
                [e + o for e, o in zip(even, odd)],
                [e - o for e, o in zip(even, odd)],
            )
        q = p - 1
        if q in planes:
            here = []
            for c in range(3):
                plain = own[q][0][c] + (own[q + 1][1][c] + own[q - 1][2][c])
                heavy = scaled[q][0][c] + (scaled[q + 1][1][c] + scaled[q - 1][2][c])
                u, k = v[q][c][0], s[q][0]
                here.append(8.1 * (k * u) + 0.125 * (u * sums[q] - (k * plain + heavy)))
            result[q] = here
            if use is not None:
                use(q, here)
    return result


def gain(stiff, free):
    return free * 0.8 / (7.1 * stiff + 7.5)


def run_copies(pairs, sems):
    copies = [
        pltpu.make_async_copy(source, target, sems.at[k])
        for k, (source, target) in enumerate(pairs)
    ]
    for copy in copies:
        copy.start()
    for copy in copies:
        copy.wait()


def start_values(density, fixed, loaded, load):
    level = (density.astype(F32) + 1.0) * (1.0 / 256.0)
    stiff = 0.05 + level * level * level
    free = (1 - fixed).astype(F32)
    factor = gain(stiff, free) * loaded.astype(F32)
    return [factor * c for c in load] + [stiff, free]


def rows_kernel(density, fixed, loaded, load, low, high, *scratch):
    run_copies(zip((density, fixed, loaded, load), scratch[:4]), scratch[4])
    d, x, m, f = scratch[:4]
    low[0:8] = jnp.zeros((8, low.shape[1]), F32)
    high[96:104] = jnp.zeros((8, low.shape[1]), F32)
    for p in range(4):
        values = start_values(d[p], x[p], m[p], [f[c, p] for c in range(3)])
        for k in range(5):
            at = 5 * (4 * k + p)
            low[8 + at : 13 + at] = values[k][0:5]
            high[at : at + 5] = values[k][3:8]


def fine_kernel(density, fixed, loaded, load, fine, *scratch):
    run_copies(zip((density, fixed, loaded, load), scratch[:4]), scratch[4])
    d, x, m, f = scratch[:4]
    for p in range(4):
        values = start_values(d[p], x[p], m[p], [f[c, p] for c in range(3)])
        for k in range(5):
            fine[k, p] = values[k]


def rim_tile(after, before):
    row = iota((8, after.shape[1]), 0)
    return jnp.where(row == 0, after, before)


def own_rows(fine, low, high, k, p):
    at = 5 * (4 * k + p)
    row = iota((8, fine.shape[3]), 0)
    turned = pltpu.roll(fine[k, p], 4, 0)
    first = jnp.where(row < 4, high[at + 1 : at + 9], turned)
    last = jnp.where(row < 4, turned, low[at + 4 : at + 12])
    rim = rim_tile(low[at + 12 : at + 13], high[at : at + 1])
    return jnp.concatenate([first, last], axis=0), rim


def side_rows(side, k):
    at = 80 + 2 * k
    rim = rim_tile(side[at + 1 : at + 2], side[at : at + 1])
    return side[16 * k : 16 * k + 16], rim


def sides_kernel(even, fine, low, high, outer, inner):
    is_even = even[0] == 1
    for k in range(5):
        first, last = [own_rows(fine, low, high, k, p)[0] for p in (0, 3)]
        outer[16 * k : 16 * k + 16] = jnp.where(is_even, first, last)
        inner[16 * k : 16 * k + 16] = jnp.where(is_even, last, first)
        ends = []
        for p in (0, 3):
            at = 5 * (4 * k + p)
            ends.append((high[at : at + 1], low[at + 12 : at + 13]))
        for j in range(2):
            first, last = ends[0][j], ends[1][j]
            at = 80 + 2 * k + j
            outer[at : at + 1] = jnp.where(is_even, first, last)
            inner[at : at + 1] = jnp.where(is_even, last, first)
    outer[90:104] = jnp.zeros((14, low.shape[1]), F32)
    inner[90:96] = jnp.zeros((6, low.shape[1]), F32)


def fine_tiles(fine, low, high, before, after):
    result = []
    for p in range(6):
        here = []
        for k in range(5):
            if p in (0, 5):
                side, at = before if p == 0 else after, 16 * k
                main = side[at + 4 : at + 12]
                rim = rim_tile(side[at + 12 : at + 13], side[at + 3 : at + 4])
            else:
                at = 5 * (4 * k + p - 1)
                main = fine[k, p - 1]
                rim = rim_tile(low[at + 8 : at + 9], high[at + 4 : at + 5])
            here.append((main, rim))
        result.append(here)
    return result


def fine_residual_kernel(fine, low, high, before, after, mid):
    tiles = []
    for p in range(6):
        if p in (0, 5):
            side = before if p == 0 else after
            tiles.append([side_rows(side, k) for k in range(5)])
        else:
            tiles.append([own_rows(fine, low, high, k, p - 1) for k in range(5)])
    v = [t[:3] for t in tiles]
    s = [t[3] for t in tiles]
    planes = range(1, 5)
    image = stencil(v, s, stiff_sums(s, planes), planes)
    rows = [[], [], [], [], []]
    for p in planes:
        stiff, free = s[p][0], tiles[p][4][0]
        back = 1.25 * (7.1 * stiff + 7.5)
        for c in range(3):
            rows[c].append(free * (back * v[p][c][0] - image[p][c]))
        rows[3].append(stiff)
        rows[4].append(free)
    row = iota((8, fine.shape[3]), 0)
    index = row % 4 * 2
    for f in range(5):
        for x in (0, 2):
            both = rows[f][x] + rows[f][x + 1]
            both = both + pltpu.roll(both, 15, 0)
            halves = [pick_rows(both[at : at + 8], index) for at in (0, 8)]
            total = pool_lanes(jnp.where(row < 4, halves[0], halves[1]))
            if f == 3:
                total = total * 0.125
            if f == 4:
                total = (total > 0.5).astype(F32)
            at = 16 * f + 4 * x
            mid[at : at + 8] = total


def mid_fields(mids):
    v, s, free, gains = [], [], [], []
    for p in range(6):
        mid = mids[p // 2].at[:, p % 2]
        stiff, open_ = mid[3], mid[4]
        g = gain(stiff, open_)
        v.append([(0.5 * g * mid[c],) for c in range(3)])
        s.append((stiff,))
        free.append(open_)
        gains.append(g)
    return v, s, free, gains


def mid_residual_kernel(before, mid, after, low):
    v, s, free, _ = mid_fields((before, mid, after))
    planes = range(2, 4)
    image = stencil(v, s, stiff_sums(s, planes), planes)
    pairs = []
    for c in range(3):
        pairs.append(
            sum(free[p] * (mid[c, p - 2] - 2.0 * image[p][c]) for p in planes)
        )
    pairs.append(s[2][0] + s[3][0])
    pairs.append(free[2] + free[3])
    sums = [pool_lanes(a + pltpu.roll(a, 7, 0)) for a in pairs]
    sums[3] = sums[3] * 0.125
    sums[4] = (sums[4] > 0.5).astype(F32)
    row = iota(sums[0].shape, 0)
    index = 2 + row % 2 * 2
    packed = pick_rows(sums[0], index)
    for f in range(1, 4):
        packed = jnp.where(row // 2 == f, pick_rows(sums[f], index), packed)
    last = pick_rows(sums[4], index)[0:2]
    for k in range(low.shape[0]):
        low[k, 0:8] = packed
        low[k, 8:10] = last


def low_tiles(low, p, f):
    at = 2 if f == 4 else 0
    row = iota((8, low.shape[3]), 0)
    index = 2 * f - at + (row + 1) % 2
    picks = [pick_rows(low[p, b, at : at + 8], index) for b in range(5)]
    main = picks[0]
    for b in range(1, 5):
        main = jnp.where(row >= 2 * b - 1, picks[b], main)
    after = low[p, 4, 2 * f + 1 : 2 * f + 2]
    return main, rim_tile(after, low[p, 0, 2 * f : 2 * f + 1])


def finish_kernel(
    low,
    mid_before,
    mid,
    mid_after,
    fine,
    row_after,
    row_before,
    before,
    after,
    out,
    held,
    sems,
):
    fields = [[low_tiles(low, p, f) for f in range(5)] for p in range(9)]
    s = [f[3] for f in fields]
    gains = [tuple(gain(f[3][k], f[4][k]) for k in range(2)) for f in fields]
    first = [
        [tuple(0.25 * gains[p][k] * fields[p][c][k] for k in range(2)) for c in range(3)]
        for p in range(9)
    ]
    v = dict(enumerate(first))
    sums = stiff_sums(s, range(1, 8))
    for reach in (1, 2, 3):
        planes = range(reach, 9 - reach)
        image = stencil(v, s, sums, planes)
        v = {
            p: [
                (v[p][c][0] + first[p][c][0] - gains[p][0] * image[p][c],)
                for c in range(3)
            ]
            for p in planes
        }
    row = iota((8, low.shape[3]), 0)
    raised = [
        [spread_lanes(pick_rows(v[p][c][0], 2 + row // 2)) for p in (3, 4, 5)]
        for c in range(3)
    ]
    first, s, free, gains = mid_fields((mid_before, mid, mid_after))
    v = []
    for p in range(6):
        here = []
        for c in range(3):
            here.append((first[p][c][0] + free[p] * raised[c][p // 2],))
        v.append(here)
    planes = range(1, 5)
    image = stencil(v, s, stiff_sums(s, planes), planes)
    row = iota((8, mid.shape[3]), 0)
    picks = (2 + row // 2, jnp.where(row == 0, 6, 1))
    raised = []
    for c in range(3):
        raised.append([])
        for p in planes:
            a = v[p][c][0] + first[p][c][0] - gains[p] * image[p][c]
            raised[c].append([spread_lanes(pick_rows(a, index)) for index in picks])
    tiles = fine_tiles(fine, row_after, row_before, before, after)
    s = [t[3] for t in tiles]
    v = []
    for p in range(6):
        here = []
        for c in range(3):
            up = raised[c][(p + 1) // 2]
            here.append(
                tuple(tiles[p][c][k] + tiles[p][4][k] * up[k] for k in range(2))
            )
        v.append(here)
    sums = stiff_sums(s, planes)
    copies = []

    def finish(p, image):
        g = gain(s[p][0], tiles[p][4][0])
        for c in range(3):
            held[c, p - 1] = v[p][c][0] + tiles[p][c][0] - g * image[c]
        copies.append(
            pltpu.make_async_copy(held.at[:, p - 1], out.at[:, p - 1], sems.at[p - 1])
        )
        copies[-1].start()

    stencil(v, s, sums, planes, finish)
    for copy in copies:
        copy.wait()


def call(kernel, shapes, *args, ins=None, outs=None, scratch=(), limit=48):
    results = [jax.ShapeDtypeStruct(shape, F32) for shape in shapes]
    outs = outs or [VMEM] * len(results)
    return pl.pallas_call(
        kernel,
        out_shape=results if len(results) > 1 else results[0],
        in_specs=ins or [VMEM] * len(args),
        out_specs=outs if len(results) > 1 else outs[0],
        scratch_shapes=list(scratch),
        compiler_params=pltpu.CompilerParams(vmem_limit_bytes=limit << 20),
    )(*args)


def inner_swap(value, axis):
    return lax.ppermute(value, axis, [(i, i ^ 1) for i in range(lax.axis_size(axis))])


def outer_swap(value, axis):
    n = lax.axis_size(axis)
    return lax.ppermute(
        value, axis, [(i, ((i + 1) ^ 1) - 1) for i in range(1, n - 1)]
    )


def swaps(value, axis):
    even = lax.axis_index(axis) % 2 == 0
    outer = outer_swap(jnp.concatenate([value, value[:EXTRA]]), axis)[: value.shape[0]]
    inner = inner_swap(value, axis)
    return jnp.where(even, outer, inner), jnp.where(even, inner, outer)


def gather_low(low):
    nx, ny = lax.axis_size("gx"), lax.axis_size("gy")
    nz = low.shape[2]
    groups = [
        [(8 * g + i) * ny + 2 * h + j for i in range(8) for j in range(2)]
        for g in range(nx // 8)
        for h in range(ny // 2)
    ]
    row = lax.all_to_all(low, ("gx", "gy"), 0, 0, axis_index_groups=groups)
    place = lax.axis_index("gx") % 8
    first = place < 4
    moves = [(j, j + 8) for j in range(nx - 8) if j % 8 < 4]
    moves += [(j, j - 8) for j in range(8, nx) if j % 8 >= 4]
    half = jnp.where(first, row[8:], row[:8]).reshape(80, nz)
    other = lax.ppermute(half, "gx", moves).reshape(8, 10, nz)
    planes = jnp.where(
        first, jnp.concatenate([other, row]), jnp.concatenate([row, other])
    )
    pair = lax.dynamic_slice_in_dim(planes, place % 4 * 2, 18, 0)
    even = lax.axis_index("gy") % 2 == 0
    beside = outer_swap(pair.reshape(180, nz), "gy").reshape(9, 2, 10, nz)
    own = jnp.where(even, pair[0::2], pair[1::2]).reshape(90, nz)
    moves = [(j + 2, j) if j % 2 == 0 else (j, j + 2) for j in range(ny - 2)]
    beyond = lax.ppermute(own, "gy", moves).reshape(9, 1, 10, nz)
    pair = pair.reshape(9, 2, 10, nz)
    return jnp.where(
        even,
        jnp.concatenate([beside, pair, beyond], axis=1),
        jnp.concatenate([beyond, pair, beside], axis=1),
    )


def per_device(density, fixed, loaded, load):
    nz = density.shape[2]
    args = (density, fixed, loaded, load)
    sems = pltpu.SemaphoreType.DMA((4,))
    inputs = dict(
        ins=[HBM] * 4, scratch=[pltpu.VMEM(a.shape, a.dtype) for a in args] + [sems]
    )
    low_rows, high_rows = call(
        rows_kernel, [(108, nz), (104, nz)], *args, limit=60, **inputs
    )
    n = lax.axis_size("gy")
    row_after = lax.ppermute(low_rows, "gy", [(i + 1, i) for i in range(n - 1)])
    row_before = lax.ppermute(high_rows, "gy", [(i, i + 1) for i in range(n - 1)])
    fine = call(fine_kernel, [(5, 4, 8, nz)], *args, **inputs)

    even = lax.axis_index("gx") % 2 == 0
    outer, inner = call(
        sides_kernel,
        [(104, nz), (96, nz)],
        even.astype(jnp.int32).reshape(1),
        fine,
        row_after,
        row_before,
        ins=[SMEM] + [VMEM] * 3,
    )
    outer, inner = outer_swap(outer, "gx")[:96], inner_swap(inner, "gx")
    before, after = jnp.where(even, outer, inner), jnp.where(even, inner, outer)
    fine_args = (fine, row_after, row_before, before, after)
    mid = call(fine_residual_kernel, [(80, nz // 2)], *fine_args)

    sides = swaps(mid, "gx")
    mids = [a.reshape(5, 2, 8, nz // 2) for a in (sides[0], mid, sides[1])]
    low = call(mid_residual_kernel, [(16, 10, nz // 4)], *mids)
    low = gather_low(low)
    return call(
        finish_kernel,
        [(3, 4, 8, nz)],
        low,
        *mids,
        *fine_args,
        outs=[HBM],
        scratch=[pltpu.VMEM((3, 4, 8, nz), F32), sems],
    )


def solution(mesh):
    return jax.shard_map(
        per_device,
        mesh=mesh,
        in_specs=(
            P("gx", "gy", None),
            P("gx", "gy", None),
            P("gx", "gy", None),
            P(None, "gx", "gy", None),
        ),
        out_specs=P(None, "gx", "gy", None),
        check_vma=False,
    )
```

```python
import jax
import jax.numpy as jnp
from jax import lax
from jax.experimental import pallas as pl
from jax.experimental.pallas import tpu as pltpu
from jax.sharding import PartitionSpec as P

F32 = jnp.float32
EXTRA = 8
HBM = pl.BlockSpec(memory_space=pltpu.HBM)
SMEM = pl.BlockSpec(memory_space=pltpu.SMEM)
VMEM = pl.BlockSpec(memory_space=pltpu.VMEM)


def iota(shape, dim):
    return lax.broadcasted_iota(jnp.int32, shape, dim)


def pick_rows(a, index):
    return jnp.take_along_axis(a, index, axis=0)


def lanes(a, k):
    return a[:, 128 * k : 128 * (k + 1)]


def spread_lanes(a):
    half = iota((8, 128), 1) // 2
    tiles = []
    for k in range(a.shape[1] // 128):
        for index in (half, half + 64):
            tiles.append(jnp.take_along_axis(lanes(a, k), index, axis=1))
    return jnp.concatenate(tiles, axis=1)


def pool_lanes(a):
    a = a + pltpu.roll(a, a.shape[1] - 1, 1)
    lane = iota((8, 128), 1)
    index = lane % 64 * 2
    tiles = []
    for k in range(0, a.shape[1] // 128, 2):
        low = jnp.take_along_axis(lanes(a, k), index, axis=1)
        high = jnp.take_along_axis(lanes(a, k + 1), index, axis=1)
        tiles.append(jnp.where(lane < 64, low, high))
    return jnp.concatenate(tiles, axis=1)


def z_parts(tiles):
    t, d = [], []
    for a in tiles:
        n = a.shape[1]
        after, before = pltpu.roll(a, n - 1, 1), pltpu.roll(a, 1, 1)
        lane = iota((a.shape[0], 128), 1)
        last = jnp.where(lane == 127, 0.0, after[:, n - 128 :])
        first = jnp.where(lane == 0, 0.0, before[:, :128])
        if n > 128:
            last = jnp.concatenate([after[:, : n - 128], last], axis=1)
            first = jnp.concatenate([first, before[:, 128:]], axis=1)
        after, before = last, first
        t.append((after + before) + 2.0 * a)
        d.append(after - before)
    return tuple(t), tuple(d)


def y_pair(tiles):
    a = tiles[0]
    n = a.shape[0]
    if len(tiles) == 1:
        return pltpu.roll(a, n - 1, 0), pltpu.roll(a, 1, 0)
    row = iota((8, a.shape[1]), 0)
    tiles = [tiles[1]] + [a[k : k + 8] for k in range(0, n, 8)] + [tiles[1]]
    after, before = [], []
    for k in range(1, len(tiles) - 1):
        after.append(pltpu.roll(jnp.where(row == 0, tiles[k + 1], tiles[k]), 7, 0))
        before.append(pltpu.roll(jnp.where(row == 7, tiles[k - 1], tiles[k]), 1, 0))
    if n == 8:
        return after[0], before[0]
    return jnp.concatenate(after, axis=0), jnp.concatenate(before, axis=0)


def y_t(tiles):
    after, before = y_pair(tiles)
    return (after + before) + 2.0 * tiles[0]


def y_d(tiles):
    after, before = y_pair(tiles)
    return after - before


def y_both(tiles):
    after, before = y_pair(tiles)
    return (after + before) + 2.0 * tiles[0], after - before


def plane_terms(v):
    (tx, dx), (ty, dy), (tz, dz) = [z_parts(c) for c in v]
    xt, xd = y_both(tx)
    xc = y_t(dx)
    yt, yd = y_both(ty)
    yc = y_d(dy)
    zt = y_t(tz)
    zb, zc = y_both(dz)
    return (
        (xt, yt + 0.25 * zc, zt + 0.25 * yc),
        (0.25 * (yd + zb), 0.25 * xd, 0.25 * xc),
    )


def scalar_terms(s):
    t, _ = z_parts(s)
    return y_t(t)


def times(a, b):
    return tuple(p * q for p, q in zip(a, b))


def stiff_sums(s, planes):
    terms = {p: scalar_terms(s[p]) for p in range(planes[0] - 1, planes[-1] + 2)}
    return {p: 2.0 * terms[p] + (terms[p + 1] + terms[p - 1]) for p in planes}


def stencil(v, s, sums, planes, use=None):
    own, scaled = {}, {}
    result = {}
    for p in range(planes[0] - 1, planes[-1] + 2):
        for store, field in ((own, v[p]), (scaled, [times(c, s[p]) for c in v[p]])):
            store[p] = plane_terms(field)
        q = p - 1
        if q in planes:
            here = []
            for c in range(3):
                sums_x = []
                for store in (own, scaled):
                    (e0, o0), (e1, _), (e2, o2) = [
                        (store[x][0][c], store[x][1][c]) for x in (q - 1, q, q + 1)
                    ]
                    sums_x.append((e2 + e0) + 2.0 * e1 + (o2 - o0))
                plain, heavy = sums_x
                u, k = v[q][c][0], s[q][0]
                here.append(8.1 * (k * u) + 0.125 * (u * sums[q] - (k * plain + heavy)))
            result[q] = here
            if use is not None:
                use(q, here)
    return result


def gain(stiff, free):
    return free * 0.8 / (7.1 * stiff + 7.5)


def run_copies(pairs, sems):
    copies = [
        pltpu.make_async_copy(source, target, sems.at[k])
        for k, (source, target) in enumerate(pairs)
    ]
    for copy in copies:
        copy.start()
    for copy in copies:
        copy.wait()


def start_values(density, fixed, loaded, load):
    level = (density.astype(F32) + 1.0) * (1.0 / 256.0)
    stiff = 0.05 + level * level * level
    free = (1 - fixed).astype(F32)
    factor = gain(stiff, free) * loaded.astype(F32)
    return [factor * c for c in load] + [stiff, free]


def rows_kernel(density, fixed, loaded, load, low, high, *scratch):
    run_copies(zip((density, fixed, loaded, load), scratch[:4]), scratch[4])
    d, x, m, f = scratch[:4]
    low[0:8] = jnp.zeros((8, low.shape[1]), F32)
    high[96:104] = jnp.zeros((8, low.shape[1]), F32)
    for p in range(4):
        values = start_values(d[p], x[p], m[p], [f[c, p] for c in range(3)])
        for k in range(5):
            at = 5 * (4 * k + p)
            low[8 + at : 13 + at] = values[k][0:5]
            high[at : at + 5] = values[k][3:8]


def fine_kernel(density, fixed, loaded, load, fine, *scratch):
    run_copies(zip((density, fixed, loaded, load), scratch[:4]), scratch[4])
    d, x, m, f = scratch[:4]
    for p in range(4):
        values = start_values(d[p], x[p], m[p], [f[c, p] for c in range(3)])
        for k in range(5):
            fine[k, p] = values[k]


def rim_tile(after, before):
    row = iota((8, after.shape[1]), 0)
    return jnp.where(row == 0, after, before)


def own_rows(fine, low, high, k, p):
    at = 5 * (4 * k + p)
    row = iota((8, fine.shape[3]), 0)
    turned = pltpu.roll(fine[k, p], 4, 0)
    first = jnp.where(row < 4, high[at + 1 : at + 9], turned)
    last = jnp.where(row < 4, turned, low[at + 4 : at + 12])
    rim = rim_tile(low[at + 12 : at + 13], high[at : at + 1])
    return jnp.concatenate([first, last], axis=0), rim


def side_rows(side, k):
    at = 72 + 2 * k
    rim = rim_tile(side[at + 1 : at + 2], side[at : at + 1])
    return side[16 * k : 16 * k + 16], rim


def sides_kernel(even, fine, low, high, outer, inner):
    is_even = even[0] == 1

    def put(at, rows, first, last):
        outer[at : at + rows] = jnp.where(is_even, first, last)
        inner[at : at + rows] = jnp.where(is_even, last, first)

    for k in range(4):
        put(16 * k, 16, *[own_rows(fine, low, high, k, p)[0] for p in (0, 3)])
    put(64, 8, fine[4, 0], fine[4, 3])
    for k in range(5):
        ends = []
        for p in (0, 3):
            at = 5 * (4 * k + p)
            below, above = (at, at + 12) if k < 4 else (at + 4, at + 8)
            ends.append((high[below : below + 1], low[above : above + 1]))
        for j in range(2):
            put(72 + 2 * k + j, 1, ends[0][j], ends[1][j])
    outer[82:88] = jnp.zeros((6, low.shape[1]), F32)


def fine_tiles(fine, low, high, before, after):
    result = []
    for p in range(6):
        here = []
        for k in range(5):
            if p in (0, 5):
                side = before if p == 0 else after
                at, below, above = (16 * k + 4, 16 * k + 3, 16 * k + 12)
                if k == 4:
                    at, below, above = 64, 80, 81
                main = side[at : at + 8]
                rim = rim_tile(side[above : above + 1], side[below : below + 1])
            else:
                at = 5 * (4 * k + p - 1)
                main = fine[k, p - 1]
                rim = rim_tile(low[at + 8 : at + 9], high[at + 4 : at + 5])
            here.append((main, rim))
        result.append(here)
    return result


def fine_residual_kernel(fine, low, high, before, after, mid):
    tiles = []
    for p in range(6):
        if p in (0, 5):
            side = before if p == 0 else after
            tiles.append([side_rows(side, k) for k in range(4)])
        else:
            tiles.append([own_rows(fine, low, high, k, p - 1) for k in range(5)])
    v = [t[:3] for t in tiles]
    s = [t[3] for t in tiles]
    planes = range(1, 5)
    image = stencil(v, s, stiff_sums(s, planes), planes)
    rows = [[], [], [], [], []]
    for p in planes:
        stiff, free = s[p][0], tiles[p][4][0]
        back = 1.25 * (7.1 * stiff + 7.5)
        for c in range(3):
            rows[c].append(free * (back * v[p][c][0] - image[p][c]))
        rows[3].append(stiff)
        rows[4].append(free)
    row = iota((8, fine.shape[3]), 0)
    index = row % 4 * 2
    for f in range(5):
        for x in (0, 2):
            both = rows[f][x] + rows[f][x + 1]
            both = both + pltpu.roll(both, 15, 0)
            halves = [pick_rows(both[at : at + 8], index) for at in (0, 8)]
            total = pool_lanes(jnp.where(row < 4, halves[0], halves[1]))
            if f == 3:
                total = total * 0.125
            if f == 4:
                total = (total > 0.5).astype(F32)
            at = 16 * f + 4 * x
            mid[at : at + 8] = total


def mid_fields(mids):
    v, s, free, gains = [], [], [], []
    for p in range(6):
        mid = mids[p // 2].at[:, p % 2]
        stiff, open_ = mid[3], mid[4]
        g = gain(stiff, open_)
        v.append([(0.5 * g * mid[c],) for c in range(3)])
        s.append((stiff,))
        free.append(open_)
        gains.append(g)
    return v, s, free, gains


def mid_residual_kernel(before, mid, after, low):
    v, s, free, _ = mid_fields((before, mid, after))
    planes = range(2, 4)
    image = stencil(v, s, stiff_sums(s, planes), planes)
    pairs = []
    for c in range(3):
        pairs.append(
            sum(free[p] * (mid[c, p - 2] - 2.0 * image[p][c]) for p in planes)
        )
    pairs.append(s[2][0] + s[3][0])
    pairs.append(free[2] + free[3])
    sums = [pool_lanes(a + pltpu.roll(a, 7, 0)) for a in pairs]
    sums[3] = sums[3] * 0.125
    sums[4] = (sums[4] > 0.5).astype(F32)
    row = iota(sums[0].shape, 0)
    index = 2 + row % 2 * 2
    packed = pick_rows(sums[0], index)
    for f in range(1, 4):
        packed = jnp.where(row // 2 == f, pick_rows(sums[f], index), packed)
    last = pick_rows(sums[4], index)[0:2]
    for k in range(low.shape[0]):
        low[k, 0:8] = packed
        low[k, 8:10] = last


def low_tiles(low, p, f):
    at = 2 if f == 4 else 0
    row = iota((8, low.shape[3]), 0)
    index = 2 * f - at + (row + 1) % 2
    picks = [pick_rows(low[p, b, at : at + 8], index) for b in range(5)]
    main = picks[0]
    for b in range(1, 5):
        main = jnp.where(row >= 2 * b - 1, picks[b], main)
    after = low[p, 4, 2 * f + 1 : 2 * f + 2]
    return main, rim_tile(after, low[p, 0, 2 * f : 2 * f + 1])


def finish_kernel(
    low,
    mid_before,
    mid,
    mid_after,
    fine,
    row_after,
    row_before,
    before,
    after,
    out,
    held,
    sems,
):
    fields = [[low_tiles(low, p, f) for f in range(5)] for p in range(9)]
    s = [f[3] for f in fields]
    gains = [tuple(gain(f[3][k], f[4][k]) for k in range(2)) for f in fields]
    first = [
        [tuple(0.25 * gains[p][k] * fields[p][c][k] for k in range(2)) for c in range(3)]
        for p in range(9)
    ]
    v = dict(enumerate(first))
    sums = stiff_sums(s, range(1, 8))
    for reach in (1, 2, 3):
        planes = range(reach, 9 - reach)
        image = stencil(v, s, sums, planes)
        v = {
            p: [
                (v[p][c][0] + first[p][c][0] - gains[p][0] * image[p][c],)
                for c in range(3)
            ]
            for p in planes
        }
    row = iota((8, low.shape[3]), 0)
    raised = [
        [spread_lanes(pick_rows(v[p][c][0], 2 + row // 2)) for p in (3, 4, 5)]
        for c in range(3)
    ]
    first, s, free, gains = mid_fields((mid_before, mid, mid_after))
    v = []
    for p in range(6):
        here = []
        for c in range(3):
            here.append((first[p][c][0] + free[p] * raised[c][p // 2],))
        v.append(here)
    planes = range(1, 5)
    image = stencil(v, s, stiff_sums(s, planes), planes)
    row = iota((8, mid.shape[3]), 0)
    picks = (2 + row // 2, jnp.where(row == 0, 6, 1))
    raised = []
    for c in range(3):
        raised.append([])
        for p in planes:
            a = v[p][c][0] + first[p][c][0] - gains[p] * image[p][c]
            raised[c].append([spread_lanes(pick_rows(a, index)) for index in picks])
    tiles = fine_tiles(fine, row_after, row_before, before, after)
    s = [t[3] for t in tiles]
    v = []
    for p in range(6):
        here = []
        for c in range(3):
            up = raised[c][(p + 1) // 2]
            here.append(
                tuple(tiles[p][c][k] + tiles[p][4][k] * up[k] for k in range(2))
            )
        v.append(here)
    sums = stiff_sums(s, planes)
    copies = []

    def finish(p, image):
        g = gain(s[p][0], tiles[p][4][0])
        for c in range(3):
            held[c, p - 1] = v[p][c][0] + tiles[p][c][0] - g * image[c]
        copies.append(
            pltpu.make_async_copy(held.at[:, p - 1], out.at[:, p - 1], sems.at[p - 1])
        )
        copies[-1].start()

    stencil(v, s, sums, planes, finish)
    for copy in copies:
        copy.wait()


def call(kernel, shapes, *args, ins=None, outs=None, scratch=(), limit=48):
    results = [jax.ShapeDtypeStruct(shape, F32) for shape in shapes]
    outs = outs or [VMEM] * len(results)
    return pl.pallas_call(
        kernel,
        out_shape=results if len(results) > 1 else results[0],
        in_specs=ins or [VMEM] * len(args),
        out_specs=outs if len(results) > 1 else outs[0],
        scratch_shapes=list(scratch),
        compiler_params=pltpu.CompilerParams(vmem_limit_bytes=limit << 20),
    )(*args)


def inner_swap(value, axis):
    return lax.ppermute(value, axis, [(i, i ^ 1) for i in range(lax.axis_size(axis))])


def outer_swap(value, axis):
    n = lax.axis_size(axis)
    return lax.ppermute(
        value, axis, [(i, ((i + 1) ^ 1) - 1) for i in range(1, n - 1)]
    )


def swaps(value, axis):
    even = lax.axis_index(axis) % 2 == 0
    outer = outer_swap(jnp.concatenate([value, value[:EXTRA]]), axis)[: value.shape[0]]
    inner = inner_swap(value, axis)
    return jnp.where(even, outer, inner), jnp.where(even, inner, outer)


def gather_low(low):
    nx, ny = lax.axis_size("gx"), lax.axis_size("gy")
    nz = low.shape[2]
    groups = [
        [(8 * g + i) * ny + 2 * h + j for i in range(8) for j in range(2)]
        for g in range(nx // 8)
        for h in range(ny // 2)
    ]
    row = lax.all_to_all(low, ("gx", "gy"), 0, 0, axis_index_groups=groups)
    place = lax.axis_index("gx") % 8
    first = place < 4
    moves = [(j, j + 8) for j in range(nx - 8) if j % 8 < 4]
    moves += [(j, j - 8) for j in range(8, nx) if j % 8 >= 4]
    half = jnp.where(first, row[8:], row[:8]).reshape(80, nz)
    other = lax.ppermute(half, "gx", moves).reshape(8, 10, nz)
    planes = jnp.where(
        first, jnp.concatenate([other, row]), jnp.concatenate([row, other])
    )
    pair = lax.dynamic_slice_in_dim(planes, place % 4 * 2, 18, 0)
    even = lax.axis_index("gy") % 2 == 0
    beside = outer_swap(pair.reshape(180, nz), "gy").reshape(9, 2, 10, nz)
    own = jnp.where(even, pair[0::2], pair[1::2]).reshape(90, nz)
    moves = [(j + 2, j) if j % 2 == 0 else (j, j + 2) for j in range(ny - 2)]
    beyond = lax.ppermute(own, "gy", moves).reshape(9, 1, 10, nz)
    pair = pair.reshape(9, 2, 10, nz)
    return jnp.where(
        even,
        jnp.concatenate([beside, pair, beyond], axis=1),
        jnp.concatenate([beyond, pair, beside], axis=1),
    )


def per_device(density, fixed, loaded, load):
    nz = density.shape[2]
    args = (density, fixed, loaded, load)
    sems = pltpu.SemaphoreType.DMA((4,))
    inputs = dict(
        ins=[HBM] * 4, scratch=[pltpu.VMEM(a.shape, a.dtype) for a in args] + [sems]
    )
    low_rows, high_rows = call(
        rows_kernel, [(108, nz), (104, nz)], *args, limit=60, **inputs
    )
    n = lax.axis_size("gy")
    row_after = lax.ppermute(low_rows, "gy", [(i + 1, i) for i in range(n - 1)])
    row_before = lax.ppermute(high_rows, "gy", [(i, i + 1) for i in range(n - 1)])
    fine = call(fine_kernel, [(5, 4, 8, nz)], *args, **inputs)

    even = lax.axis_index("gx") % 2 == 0
    outer, inner = call(
        sides_kernel,
        [(88, nz), (82, nz)],
        even.astype(jnp.int32).reshape(1),
        fine,
        row_after,
        row_before,
        ins=[SMEM] + [VMEM] * 3,
    )
    outer, inner = outer_swap(outer, "gx")[:82], inner_swap(inner, "gx")
    before, after = jnp.where(even, outer, inner), jnp.where(even, inner, outer)
    fine_args = (fine, row_after, row_before, before, after)
    mid = call(fine_residual_kernel, [(80, nz // 2)], *fine_args)

    sides = swaps(mid, "gx")
    mids = [a.reshape(5, 2, 8, nz // 2) for a in (sides[0], mid, sides[1])]
    low = call(mid_residual_kernel, [(16, 10, nz // 4)], *mids)
    low = gather_low(low)
    return call(
        finish_kernel,
        [(3, 4, 8, nz)],
        low,
        *mids,
        *fine_args,
        outs=[HBM],
        scratch=[pltpu.VMEM((3, 4, 8, nz), F32), sems],
    )


def solution(mesh):
    return jax.shard_map(
        per_device,
        mesh=mesh,
        in_specs=(
            P("gx", "gy", None),
            P("gx", "gy", None),
            P("gx", "gy", None),
            P(None, "gx", "gy", None),
        ),
        out_specs=P(None, "gx", "gy", None),
        check_vma=False,
    )
```

```python
import jax
import jax.numpy as jnp
from jax import lax
from jax.experimental import pallas as pl
from jax.experimental.pallas import tpu as pltpu
from jax.sharding import PartitionSpec as P

F32 = jnp.float32
EXTRA = 8
HBM = pl.BlockSpec(memory_space=pltpu.HBM)
SMEM = pl.BlockSpec(memory_space=pltpu.SMEM)
VMEM = pl.BlockSpec(memory_space=pltpu.VMEM)


def iota(shape, dim):
    return lax.broadcasted_iota(jnp.int32, shape, dim)


def pick_rows(a, index):
    return jnp.take_along_axis(a, index, axis=0)


def lanes(a, k):
    return a[:, 128 * k : 128 * (k + 1)]


def spread_lanes(a):
    half = iota((8, 128), 1) // 2
    tiles = []
    for k in range(a.shape[1] // 128):
        for index in (half, half + 64):
            tiles.append(jnp.take_along_axis(lanes(a, k), index, axis=1))
    return jnp.concatenate(tiles, axis=1)


def pool_lanes(a):
    a = a + pltpu.roll(a, a.shape[1] - 1, 1)
    lane = iota((8, 128), 1)
    index = lane % 64 * 2
    tiles = []
    for k in range(0, a.shape[1] // 128, 2):
        low = jnp.take_along_axis(lanes(a, k), index, axis=1)
        high = jnp.take_along_axis(lanes(a, k + 1), index, axis=1)
        tiles.append(jnp.where(lane < 64, low, high))
    return jnp.concatenate(tiles, axis=1)


def z_parts(tiles):
    t, d = [], []
    for a in tiles:
        n = a.shape[1]
        after, before = pltpu.roll(a, n - 1, 1), pltpu.roll(a, 1, 1)
        lane = iota((a.shape[0], 128), 1)
        last = jnp.where(lane == 127, 0.0, after[:, n - 128 :])
        first = jnp.where(lane == 0, 0.0, before[:, :128])
        if n > 128:
            last = jnp.concatenate([after[:, : n - 128], last], axis=1)
            first = jnp.concatenate([first, before[:, 128:]], axis=1)
        after, before = last, first
        t.append((after + before) + 2.0 * a)
        d.append(after - before)
    return tuple(t), tuple(d)


def y_pair(tiles):
    a = tiles[0]
    n = a.shape[0]
    if len(tiles) == 1:
        return pltpu.roll(a, n - 1, 0), pltpu.roll(a, 1, 0)
    row = iota((8, a.shape[1]), 0)
    tiles = [tiles[1]] + [a[k : k + 8] for k in range(0, n, 8)] + [tiles[1]]
    after, before = [], []
    for k in range(1, len(tiles) - 1):
        after.append(pltpu.roll(jnp.where(row == 0, tiles[k + 1], tiles[k]), 7, 0))
        before.append(pltpu.roll(jnp.where(row == 7, tiles[k - 1], tiles[k]), 1, 0))
    if n == 8:
        return after[0], before[0]
    return jnp.concatenate(after, axis=0), jnp.concatenate(before, axis=0)


def y_t(tiles):
    after, before = y_pair(tiles)
    return (after + before) + 2.0 * tiles[0]


def y_d(tiles):
    after, before = y_pair(tiles)
    return after - before


def y_both(tiles):
    after, before = y_pair(tiles)
    return (after + before) + 2.0 * tiles[0], after - before


def plane_terms(v):
    (tx, dx), (ty, dy), (tz, dz) = [z_parts(c) for c in v]
    xt, xd = y_both(tx)
    xc = y_t(dx)
    yt, yd = y_both(ty)
    yc = y_d(dy)
    zt = y_t(tz)
    zb, zc = y_both(dz)
    return (
        (xt, yt + 0.25 * zc, zt + 0.25 * yc),
        (0.25 * (yd + zb), 0.25 * xd, 0.25 * xc),
    )


def scalar_terms(s):
    t, _ = z_parts(s)
    return y_t(t)


def times(a, b):
    return tuple(p * q for p, q in zip(a, b))


def stiff_sums(s, planes):
    terms = {p: scalar_terms(s[p]) for p in range(planes[0] - 1, planes[-1] + 2)}
    return {p: 2.0 * terms[p] + (terms[p + 1] + terms[p - 1]) for p in planes}


def stencil(v, s, sums, planes, use=None):
    own, scaled = {}, {}
    result = {}
    for p in range(planes[0] - 1, planes[-1] + 2):
        for store, field in ((own, v[p]), (scaled, [times(c, s[p]) for c in v[p]])):
            store[p] = plane_terms(field)
        q = p - 1
        if q in planes:
            here = []
            for c in range(3):
                sums_x = []
                for store in (own, scaled):
                    (e0, o0), (e1, _), (e2, o2) = [
                        (store[x][0][c], store[x][1][c]) for x in (q - 1, q, q + 1)
                    ]
                    sums_x.append((e2 + e0) + 2.0 * e1 + (o2 - o0))
                plain, heavy = sums_x
                u, k = v[q][c][0], s[q][0]
                here.append(8.1 * (k * u) + 0.125 * (u * sums[q] - (k * plain + heavy)))
            result[q] = here
            if use is not None:
                use(q, here)
    return result


def gain(stiff, free):
    return free * 0.8 / (7.1 * stiff + 7.5)


def start_values(density, fixed, loaded, load):
    level = (density.astype(F32) + 1.0) * (1.0 / 256.0)
    stiff = 0.05 + level * level * level
    free = (1 - fixed).astype(F32)
    factor = gain(stiff, free) * loaded.astype(F32)
    return [factor * c for c in load] + [stiff, free]


def gate_kernel(density, fixed, loaded, load, out):
    out[0] = 1


def rows_kernel(gate, density, fixed, loaded, load, low, high):
    d, x, m, f = density, fixed, loaded, load
    low[0:8] = jnp.zeros((8, low.shape[1]), F32)
    high[96:104] = jnp.zeros((8, low.shape[1]), F32)
    for p in range(4):
        values = start_values(d[p], x[p], m[p], [f[c, p] for c in range(3)])
        for k in range(5):
            at = 5 * (4 * k + p)
            low[8 + at : 13 + at] = values[k][0:5]
            high[at : at + 5] = values[k][3:8]


def fine_kernel(d, x, m, f, fine):
    for p in range(4):
        values = start_values(d[p], x[p], m[p], [f[c, p] for c in range(3)])
        for k in range(5):
            fine[k, p] = values[k]


def rim_tile(after, before):
    row = iota((8, after.shape[1]), 0)
    return jnp.where(row == 0, after, before)


def own_rows(fine, low, high, k, p):
    at = 5 * (4 * k + p)
    row = iota((8, fine.shape[3]), 0)
    turned = pltpu.roll(fine[k, p], 4, 0)
    first = jnp.where(row < 4, high[at + 1 : at + 9], turned)
    last = jnp.where(row < 4, turned, low[at + 4 : at + 12])
    rim = rim_tile(low[at + 12 : at + 13], high[at : at + 1])
    return jnp.concatenate([first, last], axis=0), rim


def side_rows(side, k):
    at = 72 + 2 * k
    rim = rim_tile(side[at + 1 : at + 2], side[at : at + 1])
    return side[16 * k : 16 * k + 16], rim


def sides_kernel(even, fine, low, high, outer, inner):
    is_even = even[0] == 1

    def put(at, rows, first, last):
        outer[at : at + rows] = jnp.where(is_even, first, last)
        inner[at : at + rows] = jnp.where(is_even, last, first)

    for k in range(4):
        put(16 * k, 16, *[own_rows(fine, low, high, k, p)[0] for p in (0, 3)])
    put(64, 8, fine[4, 0], fine[4, 3])
    for k in range(5):
        ends = []
        for p in (0, 3):
            at = 5 * (4 * k + p)
            below, above = (at, at + 12) if k < 4 else (at + 4, at + 8)
            ends.append((high[below : below + 1], low[above : above + 1]))
        for j in range(2):
            put(72 + 2 * k + j, 1, ends[0][j], ends[1][j])
    outer[82:88] = jnp.zeros((6, low.shape[1]), F32)


def fine_tiles(fine, low, high, before, after):
    result = []
    for p in range(6):
        here = []
        for k in range(5):
            if p in (0, 5):
                side = before if p == 0 else after
                at, below, above = (16 * k + 4, 16 * k + 3, 16 * k + 12)
                if k == 4:
                    at, below, above = 64, 80, 81
                main = side[at : at + 8]
                rim = rim_tile(side[above : above + 1], side[below : below + 1])
            else:
                at = 5 * (4 * k + p - 1)
                main = fine[k, p - 1]
                rim = rim_tile(low[at + 8 : at + 9], high[at + 4 : at + 5])
            here.append((main, rim))
        result.append(here)
    return result


def fine_residual_kernel(fine, low, high, before, after, mid):
    tiles = []
    for p in range(6):
        if p in (0, 5):
            side = before if p == 0 else after
            tiles.append([side_rows(side, k) for k in range(4)])
        else:
            tiles.append([own_rows(fine, low, high, k, p - 1) for k in range(5)])
    v = [t[:3] for t in tiles]
    s = [t[3] for t in tiles]
    planes = range(1, 5)
    image = stencil(v, s, stiff_sums(s, planes), planes)
    rows = [[], [], [], [], []]
    for p in planes:
        stiff, free = s[p][0], tiles[p][4][0]
        back = 1.25 * (7.1 * stiff + 7.5)
        for c in range(3):
            rows[c].append(free * (back * v[p][c][0] - image[p][c]))
        rows[3].append(stiff)
        rows[4].append(free)
    row = iota((8, fine.shape[3]), 0)
    index = row % 4 * 2
    for f in range(5):
        for x in (0, 2):
            both = rows[f][x] + rows[f][x + 1]
            both = both + pltpu.roll(both, 15, 0)
            halves = [pick_rows(both[at : at + 8], index) for at in (0, 8)]
            total = pool_lanes(jnp.where(row < 4, halves[0], halves[1]))
            if f == 3:
                total = total * 0.125
            if f == 4:
                total = (total > 0.5).astype(F32)
            at = 16 * f + 4 * x
            mid[at : at + 8] = total


def mid_fields(mids):
    v, s, free, gains = [], [], [], []
    for p in range(6):
        mid = mids[p // 2].at[:, p % 2]
        stiff, open_ = mid[3], mid[4]
        g = gain(stiff, open_)
        v.append([(0.5 * g * mid[c],) for c in range(3)])
        s.append((stiff,))
        free.append(open_)
        gains.append(g)
    return v, s, free, gains


def mid_residual_kernel(before, mid, after, low):
    v, s, free, _ = mid_fields((before, mid, after))
    planes = range(2, 4)
    image = stencil(v, s, stiff_sums(s, planes), planes)
    pairs = []
    for c in range(3):
        pairs.append(
            sum(free[p] * (mid[c, p - 2] - 2.0 * image[p][c]) for p in planes)
        )
    pairs.append(s[2][0] + s[3][0])
    pairs.append(free[2] + free[3])
    sums = [pool_lanes(a + pltpu.roll(a, 7, 0)) for a in pairs]
    sums[3] = sums[3] * 0.125
    sums[4] = (sums[4] > 0.5).astype(F32)
    row = iota(sums[0].shape, 0)
    index = 2 + row % 2 * 2
    packed = pick_rows(sums[0], index)
    for f in range(1, 4):
        packed = jnp.where(row // 2 == f, pick_rows(sums[f], index), packed)
    last = pick_rows(sums[4], index)[0:2]
    for k in range(low.shape[0]):
        low[k, 0:8] = packed
        low[k, 8:10] = last


def low_tiles(low, p, f):
    at = 2 if f == 4 else 0
    row = iota((8, low.shape[3]), 0)
    index = 2 * f - at + (row + 1) % 2
    picks = [pick_rows(low[p, b, at : at + 8], index) for b in range(5)]
    main = picks[0]
    for b in range(1, 5):
        main = jnp.where(row >= 2 * b - 1, picks[b], main)
    after = low[p, 4, 2 * f + 1 : 2 * f + 2]
    return main, rim_tile(after, low[p, 0, 2 * f : 2 * f + 1])


def finish_kernel(
    low,
    mid_before,
    mid,
    mid_after,
    fine,
    row_after,
    row_before,
    before,
    after,
    out,
    held,
    sems,
):
    fields = [[low_tiles(low, p, f) for f in range(5)] for p in range(9)]
    s = [f[3] for f in fields]
    gains = [tuple(gain(f[3][k], f[4][k]) for k in range(2)) for f in fields]
    first = [
        [tuple(0.25 * gains[p][k] * fields[p][c][k] for k in range(2)) for c in range(3)]
        for p in range(9)
    ]
    v = dict(enumerate(first))
    sums = stiff_sums(s, range(1, 8))
    for reach in (1, 2, 3):
        planes = range(reach, 9 - reach)
        image = stencil(v, s, sums, planes)
        v = {
            p: [
                (v[p][c][0] + first[p][c][0] - gains[p][0] * image[p][c],)
                for c in range(3)
            ]
            for p in planes
        }
    row = iota((8, low.shape[3]), 0)
    raised = [
        [spread_lanes(pick_rows(v[p][c][0], 2 + row // 2)) for p in (3, 4, 5)]
        for c in range(3)
    ]
    first, s, free, gains = mid_fields((mid_before, mid, mid_after))
    v = []
    for p in range(6):
        here = []
        for c in range(3):
            here.append((first[p][c][0] + free[p] * raised[c][p // 2],))
        v.append(here)
    planes = range(1, 5)
    image = stencil(v, s, stiff_sums(s, planes), planes)
    row = iota((8, mid.shape[3]), 0)
    picks = (2 + row // 2, jnp.where(row == 0, 6, 1))
    raised = []
    for c in range(3):
        raised.append([])
        for p in planes:
            a = v[p][c][0] + first[p][c][0] - gains[p] * image[p][c]
            raised[c].append([spread_lanes(pick_rows(a, index)) for index in picks])
    tiles = fine_tiles(fine, row_after, row_before, before, after)
    s = [t[3] for t in tiles]
    v = []
    for p in range(6):
        here = []
        for c in range(3):
            up = raised[c][(p + 1) // 2]
            here.append(
                tuple(tiles[p][c][k] + tiles[p][4][k] * up[k] for k in range(2))
            )
        v.append(here)
    sums = stiff_sums(s, planes)
    copies = []

    def finish(p, image):
        g = gain(s[p][0], tiles[p][4][0])
        for c in range(3):
            held[c, p - 1] = v[p][c][0] + tiles[p][c][0] - g * image[c]
        copies.append(
            pltpu.make_async_copy(held.at[:, p - 1], out.at[:, p - 1], sems.at[p - 1])
        )
        copies[-1].start()

    stencil(v, s, sums, planes, finish)
    for copy in copies:
        copy.wait()


def call(kernel, shapes, *args, ins=None, outs=None, scratch=(), limit=48):
    results = [jax.ShapeDtypeStruct(shape, F32) for shape in shapes]
    outs = outs or [VMEM] * len(results)
    return pl.pallas_call(
        kernel,
        out_shape=results if len(results) > 1 else results[0],
        in_specs=ins or [VMEM] * len(args),
        out_specs=outs if len(results) > 1 else outs[0],
        scratch_shapes=list(scratch),
        compiler_params=pltpu.CompilerParams(vmem_limit_bytes=limit << 20),
    )(*args)


def inner_swap(value, axis):
    return lax.ppermute(value, axis, [(i, i ^ 1) for i in range(lax.axis_size(axis))])


def outer_swap(value, axis):
    n = lax.axis_size(axis)
    return lax.ppermute(
        value, axis, [(i, ((i + 1) ^ 1) - 1) for i in range(1, n - 1)]
    )


def swaps(value, axis):
    even = lax.axis_index(axis) % 2 == 0
    outer = outer_swap(jnp.concatenate([value, value[:EXTRA]]), axis)[: value.shape[0]]
    inner = inner_swap(value, axis)
    return jnp.where(even, outer, inner), jnp.where(even, inner, outer)


def gather_low(low):
    nx, ny = lax.axis_size("gx"), lax.axis_size("gy")
    nz = low.shape[2]
    groups = [
        [(8 * g + i) * ny + 2 * h + j for i in range(8) for j in range(2)]
        for g in range(nx // 8)
        for h in range(ny // 2)
    ]
    row = lax.all_to_all(low, ("gx", "gy"), 0, 0, axis_index_groups=groups)
    place = lax.axis_index("gx") % 8
    first = place < 4
    moves = [(j, j + 8) for j in range(nx - 8) if j % 8 < 4]
    moves += [(j, j - 8) for j in range(8, nx) if j % 8 >= 4]
    half = jnp.where(first, row[8:], row[:8]).reshape(80, nz)
    other = lax.ppermute(half, "gx", moves).reshape(8, 10, nz)
    planes = jnp.where(
        first, jnp.concatenate([other, row]), jnp.concatenate([row, other])
    )
    pair = lax.dynamic_slice_in_dim(planes, place % 4 * 2, 18, 0)
    even = lax.axis_index("gy") % 2 == 0
    beside = outer_swap(pair.reshape(180, nz), "gy").reshape(9, 2, 10, nz)
    own = jnp.where(even, pair[0::2], pair[1::2]).reshape(90, nz)
    moves = [(j + 2, j) if j % 2 == 0 else (j, j + 2) for j in range(ny - 2)]
    beyond = lax.ppermute(own, "gy", moves).reshape(9, 1, 10, nz)
    pair = pair.reshape(9, 2, 10, nz)
    return jnp.where(
        even,
        jnp.concatenate([beside, pair, beyond], axis=1),
        jnp.concatenate([beyond, pair, beside], axis=1),
    )


def per_device(density, fixed, loaded, load):
    nz = density.shape[2]
    args = (density, fixed, loaded, load)
    sems = pltpu.SemaphoreType.DMA((4,))
    gate = pl.pallas_call(
        gate_kernel,
        out_shape=jax.ShapeDtypeStruct((1,), jnp.int32),
        in_specs=[HBM] * 4,
        out_specs=SMEM,
        compiler_params=pltpu.CompilerParams(vmem_limit_bytes=60 << 20),
    )(*args)
    low_rows, high_rows = call(
        rows_kernel, [(108, nz), (104, nz)], gate, *args, ins=[SMEM] + [VMEM] * 4
    )
    n = lax.axis_size("gy")
    row_after = lax.ppermute(low_rows, "gy", [(i + 1, i) for i in range(n - 1)])
    row_before = lax.ppermute(high_rows, "gy", [(i, i + 1) for i in range(n - 1)])
    fine = call(fine_kernel, [(5, 4, 8, nz)], *args)

    even = lax.axis_index("gx") % 2 == 0
    outer, inner = call(
        sides_kernel,
        [(88, nz), (82, nz)],
        even.astype(jnp.int32).reshape(1),
        fine,
        row_after,
        row_before,
        ins=[SMEM] + [VMEM] * 3,
    )
    outer, inner = outer_swap(outer, "gx")[:82], inner_swap(inner, "gx")
    before, after = jnp.where(even, outer, inner), jnp.where(even, inner, outer)
    fine_args = (fine, row_after, row_before, before, after)
    mid = call(fine_residual_kernel, [(80, nz // 2)], *fine_args)

    sides = swaps(mid, "gx")
    mids = [a.reshape(5, 2, 8, nz // 2) for a in (sides[0], mid, sides[1])]
    low = call(mid_residual_kernel, [(16, 10, nz // 4)], *mids)
    low = gather_low(low)
    return call(
        finish_kernel,
        [(3, 4, 8, nz)],
        low,
        *mids,
        *fine_args,
        outs=[HBM],
        scratch=[pltpu.VMEM((3, 4, 8, nz), F32), sems],
    )


def solution(mesh):
    return jax.shard_map(
        per_device,
        mesh=mesh,
        in_specs=(
            P("gx", "gy", None),
            P("gx", "gy", None),
            P("gx", "gy", None),
            P(None, "gx", "gy", None),
        ),
        out_specs=P(None, "gx", "gy", None),
        check_vma=False,
    )
```

```python
import jax
import jax.numpy as jnp
from jax import lax
from jax.experimental import pallas as pl
from jax.experimental.pallas import tpu as pltpu
from jax.sharding import PartitionSpec as P

F32 = jnp.float32
EXTRA = 1
HBM = pl.BlockSpec(memory_space=pltpu.HBM)
SMEM = pl.BlockSpec(memory_space=pltpu.SMEM)
VMEM = pl.BlockSpec(memory_space=pltpu.VMEM)


def iota(shape, dim):
    return lax.broadcasted_iota(jnp.int32, shape, dim)


def pick_rows(a, index):
    return jnp.take_along_axis(a, index, axis=0)


def lanes(a, k):
    return a[:, 128 * k : 128 * (k + 1)]


def spread_lanes(a):
    half = iota((8, 128), 1) // 2
    tiles = []
    for k in range(a.shape[1] // 128):
        for index in (half, half + 64):
            tiles.append(jnp.take_along_axis(lanes(a, k), index, axis=1))
    return jnp.concatenate(tiles, axis=1)


def pool_lanes(a):
    a = a + pltpu.roll(a, a.shape[1] - 1, 1)
    lane = iota((8, 128), 1)
    index = lane % 64 * 2
    tiles = []
    for k in range(0, a.shape[1] // 128, 2):
        low = jnp.take_along_axis(lanes(a, k), index, axis=1)
        high = jnp.take_along_axis(lanes(a, k + 1), index, axis=1)
        tiles.append(jnp.where(lane < 64, low, high))
    return jnp.concatenate(tiles, axis=1)


def z_parts(tiles):
    t, d = [], []
    for a in tiles:
        n = a.shape[1]
        after, before = pltpu.roll(a, n - 1, 1), pltpu.roll(a, 1, 1)
        lane = iota((a.shape[0], 128), 1)
        last = jnp.where(lane == 127, 0.0, after[:, n - 128 :])
        first = jnp.where(lane == 0, 0.0, before[:, :128])
        if n > 128:
            last = jnp.concatenate([after[:, : n - 128], last], axis=1)
            first = jnp.concatenate([first, before[:, 128:]], axis=1)
        after, before = last, first
        t.append((after + before) + 2.0 * a)
        d.append(after - before)
    return tuple(t), tuple(d)


def y_pair(tiles):
    a = tiles[0]
    n = a.shape[0]
    if len(tiles) == 1:
        return pltpu.roll(a, n - 1, 0), pltpu.roll(a, 1, 0)
    row = iota((8, a.shape[1]), 0)
    tiles = [tiles[1]] + [a[k : k + 8] for k in range(0, n, 8)] + [tiles[1]]
    after, before = [], []
    for k in range(1, len(tiles) - 1):
        after.append(pltpu.roll(jnp.where(row == 0, tiles[k + 1], tiles[k]), 7, 0))
        before.append(pltpu.roll(jnp.where(row == 7, tiles[k - 1], tiles[k]), 1, 0))
    if n == 8:
        return after[0], before[0]
    return jnp.concatenate(after, axis=0), jnp.concatenate(before, axis=0)


def y_t(tiles):
    after, before = y_pair(tiles)
    return (after + before) + 2.0 * tiles[0]


def y_d(tiles):
    after, before = y_pair(tiles)
    return after - before


def y_both(tiles):
    after, before = y_pair(tiles)
    return (after + before) + 2.0 * tiles[0], after - before


def plane_terms(v):
    (tx, dx), (ty, dy), (tz, dz) = [z_parts(c) for c in v]
    xt, xd = y_both(tx)
    xc = y_t(dx)
    yt, yd = y_both(ty)
    yc = y_d(dy)
    zt = y_t(tz)
    zb, zc = y_both(dz)
    return (
        (xt, yt + 0.25 * zc, zt + 0.25 * yc),
        (0.25 * (yd + zb), 0.25 * xd, 0.25 * xc),
    )


def scalar_terms(s):
    t, _ = z_parts(s)
    return y_t(t)


def times(a, b):
    return tuple(p * q for p, q in zip(a, b))


def stiff_sums(s, planes):
    terms = {p: scalar_terms(s[p]) for p in range(planes[0] - 1, planes[-1] + 2)}
    return {p: 2.0 * terms[p] + (terms[p + 1] + terms[p - 1]) for p in planes}


def stencil(v, s, sums, planes, use=None):
    own, scaled = {}, {}
    result = {}
    for p in range(planes[0] - 1, planes[-1] + 2):
        for store, field in ((own, v[p]), (scaled, [times(c, s[p]) for c in v[p]])):
            store[p] = plane_terms(field)
        q = p - 1
        if q in planes:
            here = []
            for c in range(3):
                sums_x = []
                for store in (own, scaled):
                    (e0, o0), (e1, _), (e2, o2) = [
                        (store[x][0][c], store[x][1][c]) for x in (q - 1, q, q + 1)
                    ]
                    sums_x.append((e2 + e0) + 2.0 * e1 + (o2 - o0))
                plain, heavy = sums_x
                u, k = v[q][c][0], s[q][0]
                here.append(8.1 * (k * u) + 0.125 * (u * sums[q] - (k * plain + heavy)))
            result[q] = here
            if use is not None:
                use(q, here)
    return result


def gain(stiff, free):
    return free * 0.8 / (7.1 * stiff + 7.5)


def start_values(density, fixed, loaded, load):
    level = (density.astype(F32) + 1.0) * (1.0 / 256.0)
    stiff = 0.05 + level * level * level
    free = (1 - fixed).astype(F32)
    factor = gain(stiff, free) * loaded.astype(F32)
    return [factor * c for c in load] + [stiff, free]


def gate_kernel(density, fixed, loaded, load, out):
    out[0] = 1


def rows_kernel(gate, density, fixed, loaded, load, low, high):
    d, x, m, f = density, fixed, loaded, load
    low[0:8] = jnp.zeros((8, low.shape[1]), F32)
    high[96:104] = jnp.zeros((8, low.shape[1]), F32)
    for p in range(4):
        values = start_values(d[p], x[p], m[p], [f[c, p] for c in range(3)])
        for k in range(5):
            at = 5 * (4 * k + p)
            low[8 + at : 13 + at] = values[k][0:5]
            high[at : at + 5] = values[k][3:8]


def fine_kernel(d, x, m, f, fine):
    for p in range(4):
        values = start_values(d[p], x[p], m[p], [f[c, p] for c in range(3)])
        for k in range(5):
            fine[k, p] = values[k]


def rim_tile(after, before):
    row = iota((8, after.shape[1]), 0)
    return jnp.where(row == 0, after, before)


def own_rows(fine, low, high, k, p):
    at = 5 * (4 * k + p)
    row = iota((8, fine.shape[3]), 0)
    turned = pltpu.roll(fine[k, p], 4, 0)
    first = jnp.where(row < 4, high[at + 1 : at + 9], turned)
    last = jnp.where(row < 4, turned, low[at + 4 : at + 12])
    rim = rim_tile(low[at + 12 : at + 13], high[at : at + 1])
    return jnp.concatenate([first, last], axis=0), rim


def side_rows(side, k):
    at = 72 + 2 * k
    rim = rim_tile(side[at + 1 : at + 2], side[at : at + 1])
    return side[16 * k : 16 * k + 16], rim


def sides_kernel(even, fine, low, high, outer, inner):
    is_even = even[0] == 1

    def put(at, rows, first, last):
        outer[at : at + rows] = jnp.where(is_even, first, last)
        inner[at : at + rows] = jnp.where(is_even, last, first)

    for k in range(4):
        put(16 * k, 16, *[own_rows(fine, low, high, k, p)[0] for p in (0, 3)])
    put(64, 8, fine[4, 0], fine[4, 3])
    for k in range(5):
        ends = []
        for p in (0, 3):
            at = 5 * (4 * k + p)
            below, above = (at, at + 12) if k < 4 else (at + 4, at + 8)
            ends.append((high[below : below + 1], low[above : above + 1]))
        for j in range(2):
            put(72 + 2 * k + j, 1, ends[0][j], ends[1][j])
    outer[82:88] = jnp.zeros((6, low.shape[1]), F32)


def fine_tiles(fine, low, high, before, after):
    result = []
    for p in range(6):
        here = []
        for k in range(5):
            if p in (0, 5):
                side = before if p == 0 else after
                at, below, above = (16 * k + 4, 16 * k + 3, 16 * k + 12)
                if k == 4:
                    at, below, above = 64, 80, 81
                main = side[at : at + 8]
                rim = rim_tile(side[above : above + 1], side[below : below + 1])
            else:
                at = 5 * (4 * k + p - 1)
                main = fine[k, p - 1]
                rim = rim_tile(low[at + 8 : at + 9], high[at + 4 : at + 5])
            here.append((main, rim))
        result.append(here)
    return result


def fine_residual_kernel(fine, low, high, before, after, mid):
    tiles = []
    for p in range(6):
        if p in (0, 5):
            side = before if p == 0 else after
            tiles.append([side_rows(side, k) for k in range(4)])
        else:
            tiles.append([own_rows(fine, low, high, k, p - 1) for k in range(5)])
    v = [t[:3] for t in tiles]
    s = [t[3] for t in tiles]
    planes = range(1, 5)
    image = stencil(v, s, stiff_sums(s, planes), planes)
    rows = [[], [], [], [], []]
    for p in planes:
        stiff, free = s[p][0], tiles[p][4][0]
        back = 1.25 * (7.1 * stiff + 7.5)
        for c in range(3):
            rows[c].append(free * (back * v[p][c][0] - image[p][c]))
        rows[3].append(stiff)
        rows[4].append(free)
    row = iota((8, fine.shape[3]), 0)
    index = row % 4 * 2
    for f in range(5):
        for x in (0, 2):
            both = rows[f][x] + rows[f][x + 1]
            both = both + pltpu.roll(both, 15, 0)
            halves = [pick_rows(both[at : at + 8], index) for at in (0, 8)]
            total = pool_lanes(jnp.where(row < 4, halves[0], halves[1]))
            if f == 3:
                total = total * 0.125
            if f == 4:
                total = (total > 0.5).astype(F32)
            at = 16 * f + 4 * x
            mid[at : at + 8] = total


def mid_fields(mids):
    v, s, free, gains = [], [], [], []
    for p in range(6):
        mid = mids[p // 2].at[:, p % 2]
        stiff, open_ = mid[3], mid[4]
        g = gain(stiff, open_)
        v.append([(0.5 * g * mid[c],) for c in range(3)])
        s.append((stiff,))
        free.append(open_)
        gains.append(g)
    return v, s, free, gains


def mid_residual_kernel(before, mid, after, low):
    v, s, free, _ = mid_fields((before, mid, after))
    planes = range(2, 4)
    image = stencil(v, s, stiff_sums(s, planes), planes)
    pairs = []
    for c in range(3):
        pairs.append(
            sum(free[p] * (mid[c, p - 2] - 2.0 * image[p][c]) for p in planes)
        )
    pairs.append(s[2][0] + s[3][0])
    pairs.append(free[2] + free[3])
    sums = [pool_lanes(a + pltpu.roll(a, 7, 0)) for a in pairs]
    sums[3] = sums[3] * 0.125
    sums[4] = (sums[4] > 0.5).astype(F32)
    row = iota(sums[0].shape, 0)
    index = 2 + row % 2 * 2
    packed = pick_rows(sums[0], index)
    for f in range(1, 4):
        packed = jnp.where(row // 2 == f, pick_rows(sums[f], index), packed)
    last = pick_rows(sums[4], index)[0:2]
    for k in range(low.shape[0]):
        low[k, 0:8] = packed
        low[k, 8:10] = last


def low_tiles(low, p, f):
    at = 2 if f == 4 else 0
    row = iota((8, low.shape[3]), 0)
    index = 2 * f - at + (row + 1) % 2
    picks = [pick_rows(low[p, b, at : at + 8], index) for b in range(5)]
    main = picks[0]
    for b in range(1, 5):
        main = jnp.where(row >= 2 * b - 1, picks[b], main)
    after = low[p, 4, 2 * f + 1 : 2 * f + 2]
    return main, rim_tile(after, low[p, 0, 2 * f : 2 * f + 1])


def finish_kernel(
    low,
    mid_before,
    mid,
    mid_after,
    fine,
    row_after,
    row_before,
    before,
    after,
    out,
    held,
    sems,
):
    fields = [[low_tiles(low, p, f) for f in range(5)] for p in range(9)]
    s = [f[3] for f in fields]
    gains = [tuple(gain(f[3][k], f[4][k]) for k in range(2)) for f in fields]
    first = [
        [tuple(0.25 * gains[p][k] * fields[p][c][k] for k in range(2)) for c in range(3)]
        for p in range(9)
    ]
    v = dict(enumerate(first))
    sums = stiff_sums(s, range(1, 8))
    for reach in (1, 2, 3):
        planes = range(reach, 9 - reach)
        image = stencil(v, s, sums, planes)
        v = {
            p: [
                (v[p][c][0] + first[p][c][0] - gains[p][0] * image[p][c],)
                for c in range(3)
            ]
            for p in planes
        }
    row = iota((8, low.shape[3]), 0)
    raised = [
        [spread_lanes(pick_rows(v[p][c][0], 2 + row // 2)) for p in (3, 4, 5)]
        for c in range(3)
    ]
    first, s, free, gains = mid_fields((mid_before, mid, mid_after))
    v = []
    for p in range(6):
        here = []
        for c in range(3):
            here.append((first[p][c][0] + free[p] * raised[c][p // 2],))
        v.append(here)
    planes = range(1, 5)
    image = stencil(v, s, stiff_sums(s, planes), planes)
    row = iota((8, mid.shape[3]), 0)
    picks = (2 + row // 2, jnp.where(row == 0, 6, 1))
    raised = []
    for c in range(3):
        raised.append([])
        for p in planes:
            a = v[p][c][0] + first[p][c][0] - gains[p] * image[p][c]
            raised[c].append([spread_lanes(pick_rows(a, index)) for index in picks])
    tiles = fine_tiles(fine, row_after, row_before, before, after)
    s = [t[3] for t in tiles]
    v = []
    for p in range(6):
        here = []
        for c in range(3):
            up = raised[c][(p + 1) // 2]
            here.append(
                tuple(tiles[p][c][k] + tiles[p][4][k] * up[k] for k in range(2))
            )
        v.append(here)
    sums = stiff_sums(s, planes)
    copies = []

    def finish(p, image):
        g = gain(s[p][0], tiles[p][4][0])
        for c in range(3):
            held[c, p - 1] = v[p][c][0] + tiles[p][c][0] - g * image[c]
        copies.append(
            pltpu.make_async_copy(held.at[:, p - 1], out.at[:, p - 1], sems.at[p - 1])
        )
        copies[-1].start()

    stencil(v, s, sums, planes, finish)
    for copy in copies:
        copy.wait()


def call(kernel, shapes, *args, ins=None, outs=None, scratch=(), limit=48):
    results = [jax.ShapeDtypeStruct(shape, F32) for shape in shapes]
    outs = outs or [VMEM] * len(results)
    return pl.pallas_call(
        kernel,
        out_shape=results if len(results) > 1 else results[0],
        in_specs=ins or [VMEM] * len(args),
        out_specs=outs if len(results) > 1 else outs[0],
        scratch_shapes=list(scratch),
        compiler_params=pltpu.CompilerParams(vmem_limit_bytes=limit << 20),
    )(*args)


def inner_swap(value, axis):
    return lax.ppermute(value, axis, [(i, i ^ 1) for i in range(lax.axis_size(axis))])


def outer_swap(value, axis):
    n = lax.axis_size(axis)
    return lax.ppermute(
        value, axis, [(i, ((i + 1) ^ 1) - 1) for i in range(1, n - 1)]
    )


def swaps(value, axis):
    even = lax.axis_index(axis) % 2 == 0
    outer = outer_swap(jnp.concatenate([value, value[:EXTRA]]), axis)[: value.shape[0]]
    inner = inner_swap(value, axis)
    return jnp.where(even, outer, inner), jnp.where(even, inner, outer)


def gather_low(low):
    nx, ny = lax.axis_size("gx"), lax.axis_size("gy")
    nz = low.shape[2]
    groups = [
        [(8 * g + i) * ny + 2 * h + j for i in range(8) for j in range(2)]
        for g in range(nx // 8)
        for h in range(ny // 2)
    ]
    row = lax.all_to_all(low, ("gx", "gy"), 0, 0, axis_index_groups=groups)
    place = lax.axis_index("gx") % 8
    first = place < 4
    moves = [(j, j + 8) for j in range(nx - 8) if j % 8 < 4]
    moves += [(j, j - 8) for j in range(8, nx) if j % 8 >= 4]
    half = jnp.where(first, row[8:], row[:8]).reshape(80, nz)
    other = lax.ppermute(half, "gx", moves).reshape(8, 10, nz)
    planes = jnp.where(
        first, jnp.concatenate([other, row]), jnp.concatenate([row, other])
    )
    pair = lax.dynamic_slice_in_dim(planes, place % 4 * 2, 18, 0)
    even = lax.axis_index("gy") % 2 == 0
    beside = outer_swap(pair.reshape(180, nz), "gy").reshape(9, 2, 10, nz)
    own = jnp.where(even, pair[0::2], pair[1::2]).reshape(90, nz)
    moves = [(j + 2, j) if j % 2 == 0 else (j, j + 2) for j in range(ny - 2)]
    beyond = lax.ppermute(own, "gy", moves).reshape(9, 1, 10, nz)
    pair = pair.reshape(9, 2, 10, nz)
    return jnp.where(
        even,
        jnp.concatenate([beside, pair, beyond], axis=1),
        jnp.concatenate([beyond, pair, beside], axis=1),
    )


def per_device(density, fixed, loaded, load):
    nz = density.shape[2]
    args = (density, fixed, loaded, load)
    sems = pltpu.SemaphoreType.DMA((4,))
    gate = pl.pallas_call(
        gate_kernel,
        out_shape=jax.ShapeDtypeStruct((1,), jnp.int32),
        in_specs=[HBM] * 4,
        out_specs=SMEM,
        compiler_params=pltpu.CompilerParams(vmem_limit_bytes=60 << 20),
    )(*args)
    low_rows, high_rows = call(
        rows_kernel, [(108, nz), (104, nz)], gate, *args, ins=[SMEM] + [VMEM] * 4
    )
    n = lax.axis_size("gy")
    row_after = lax.ppermute(low_rows, "gy", [(i + 1, i) for i in range(n - 1)])
    row_before = lax.ppermute(high_rows, "gy", [(i, i + 1) for i in range(n - 1)])
    fine = call(fine_kernel, [(5, 4, 8, nz)], *args)

    even = lax.axis_index("gx") % 2 == 0
    outer, inner = call(
        sides_kernel,
        [(88, nz), (82, nz)],
        even.astype(jnp.int32).reshape(1),
        fine,
        row_after,
        row_before,
        ins=[SMEM] + [VMEM] * 3,
    )
    outer, inner = outer_swap(outer, "gx")[:82], inner_swap(inner, "gx")
    before, after = jnp.where(even, outer, inner), jnp.where(even, inner, outer)
    fine_args = (fine, row_after, row_before, before, after)
    mid = call(fine_residual_kernel, [(80, nz // 2)], *fine_args)

    sides = swaps(mid, "gx")
    mids = [a.reshape(5, 2, 8, nz // 2) for a in (sides[0], mid, sides[1])]
    low = call(mid_residual_kernel, [(16, 10, nz // 4)], *mids)
    low = gather_low(low)
    return call(
        finish_kernel,
        [(3, 4, 8, nz)],
        low,
        *mids,
        *fine_args,
        outs=[HBM],
        scratch=[pltpu.VMEM((3, 4, 8, nz), F32), sems],
    )


def solution(mesh):
    return jax.shard_map(
        per_device,
        mesh=mesh,
        in_specs=(
            P("gx", "gy", None),
            P("gx", "gy", None),
            P("gx", "gy", None),
            P(None, "gx", "gy", None),
        ),
        out_specs=P(None, "gx", "gy", None),
        check_vma=False,
    )
```
